128 devices in a mesh: fsdp: 32 (over x, z_hi, y), seq: 4 (over z_lo, core).
Axes of the slice: x: 4, y: 4, z: 4 (z_hi: 2, z_lo: 2; z = z_hi * 2 + z_lo), core: 2. Of those that a mesh axis runs over, the one named last changes fastest.
Arguments:
- clips: bfloat16 [32, 16, 64, 768], P('fsdp', 'seq'), may hold values from -6 to 6
- norm_gain: bfloat16 [2, 3, 768], P(None, None, 'fsdp'), may hold values from 0.099609375 to 1.8984375
- norm_bias: bfloat16 [2, 3, 768], P(None, None, 'fsdp'), may hold values from -2 to 2
- qkv_weight: bfloat16 [2, 2, 768, 2304], P(None, None, 'fsdp'), may hold values from -0.21875 to 0.21875
- qkv_bias: bfloat16 [2, 2, 2, 768], P(None, None, None, 'fsdp'), may hold values from -2 to 2
- out_weight: bfloat16 [2, 2, 768, 768], P(None, None, 'fsdp'), may hold values from -0.875 to 0.875
- out_bias: bfloat16 [2, 2, 768], P(None, None, 'fsdp'), may hold values from -2 to 2
- up_weight: bfloat16 [2, 768, 3072], P(None, 'fsdp'), may hold values from -0.21875 to 0.21875
- up_bias: bfloat16 [2, 3072], P(None, 'fsdp'), may hold values from -3 to 3
- down_weight: bfloat16 [2, 3072, 768], P(None, 'fsdp'), may hold values from -0.109375 to 0.109375
- down_bias: bfloat16 [2, 768], P(None, 'fsdp'), may hold values from -2 to 2
- cotangent: bfloat16 [32, 16, 64, 768], P('fsdp', 'seq'), may hold values from -6 to 6
Outputs:
- layer_output: bfloat16 [32, 16, 64, 768], P('fsdp', 'seq')
- clips_grad: bfloat16 [32, 16, 64, 768], P('fsdp', 'seq')
- norm_gain_grad: float32 [2, 3, 768], P(None, None, 'fsdp')
- norm_bias_grad: float32 [2, 3, 768], P(None, None, 'fsdp')
- qkv_weight_grad: float32 [2, 2, 768, 2304], P(None, None, 'fsdp')
- qkv_bias_grad: float32 [2, 2, 2, 768], P(None, None, None, 'fsdp')
- out_weight_grad: float32 [2, 2, 768, 768], P(None, None, 'fsdp')
- out_bias_grad: float32 [2, 2, 768], P(None, None, 'fsdp')
- up_weight_grad: float32 [2, 768, 3072], P(None, 'fsdp')
- up_bias_grad: float32 [2, 3072], P(None, 'fsdp')
- down_weight_grad: float32 [2, 3072, 768], P(None, 'fsdp')
- down_bias_grad: float32 [2, 768], P(None, 'fsdp')
The draws below stay inside these ranges and needn't reach their ends.
All inputs are finite; a program needn't handle non-finite values.
Results may differ from the reference program's by a relative error of at most 0.02.
Values may be sent and summed in bfloat16 or wider, within the bound.
A program may use at most 256 MiB of HBM per device.

```python
import jax
import jax.numpy as jnp
from jax import lax

D = 768
HEADS = 12
HEAD_DIM = 64
FF = 3072
FRAMES = 16
PLACES = 64
LAYERS = 2
CLIPS = 32


def spiked(array, key, source, target, shards_of, factor):
    owner, partner = [(jnp.arange(array.shape[position]) // (array.shape[position] // shards_of)).reshape([-1 if axis == position else 1 for axis in range(array.ndim)]) for position in (source, target)]
    chosen = jax.random.permutation(key, shards_of)[partner]
    strong = (owner == chosen) | (owner == (partner + shards_of // 2) % shards_of)
    return jnp.where(strong, factor * array, array)


def levels(stream_key, shape, pieces, low, top_value):
    level = 1.0
    for axis_at, blocks in pieces:
        steps = jax.random.uniform(jax.random.fold_in(jax.random.fold_in(stream_key, 6), axis_at), (blocks,), jnp.float32, low / len(pieces), top_value / len(pieces))
        level = level * jnp.repeat(jnp.exp(steps), shape[axis_at] // blocks).reshape((-1,) + (1,) * (len(shape) - 1 - axis_at))
    return level


def noise(key, shape, deviation, bound, cuts=(), held_as=jnp.bfloat16):
    factor_of = levels(key, shape, cuts, -0.22, 0.18) if cuts else 1.0
    values = jax.random.normal(key, shape, jnp.float32) * deviation * factor_of
    return jnp.minimum(jnp.maximum(values, -bound), bound).astype(held_as)


def noise_with(stream_key, shape, deviation, limit, pieces, heavy, held_as=jnp.bfloat16):
    drawn = deviation * jax.random.normal(stream_key, shape, jnp.float32)
    if pieces:
        drawn = drawn * levels(stream_key, shape, pieces, -0.22, 0.18)
    return jnp.clip(spiked(drawn, jax.random.fold_in(stream_key, 3), *heavy), -limit, limit).astype(held_as)


def setup_inputs(seed: int = 0) -> dict:
    key_list = jax.random.split(jax.random.key(seed), 13)
    return {
        "clips": noise(key_list[0], (CLIPS, FRAMES, PLACES, D), 1.0, 6.0, ((0, 32), (1, 4))),
        "norm_gain": jnp.clip(1.0 + 0.18 * jax.random.normal(key_list[1], (LAYERS, 3, D), jnp.float32), 0.099609375, 1.8984375).astype(jnp.bfloat16),
        "norm_bias": noise(key_list[2], (LAYERS, 3, D), 0.3, 2.0, ((2, 32),)),
        "qkv_weight": noise(key_list[3], (LAYERS, 2, D, 3 * D), D ** -0.5, 0.21875, ((2, 32),)),
        "qkv_bias": noise(key_list[4], (LAYERS, 2, 2, D), 0.3, 2.0, ((3, 32),)),
        "out_weight": noise(key_list[5], (LAYERS, 2, D, D), (D // 16) ** -0.5, 0.875, ((2, 32),)),
        "out_bias": noise(key_list[6], (LAYERS, 2, D), 0.3, 2.0, ((2, 32),)),
        "up_weight": noise(key_list[7], (LAYERS, D, FF), D ** -0.5, 0.21875, ((1, 32),)),
        "up_bias": noise(key_list[8], (LAYERS, FF), 0.5, 3.0, ((1, 32),)),
        "down_weight": noise(key_list[9], (LAYERS, FF, D), FF ** -0.5, 0.109375, ((1, 32),)),
        "down_bias": noise(key_list[10], (LAYERS, D), 0.3, 2.0, ((1, 32),)),
        "cotangent": noise_with(key_list[11], (CLIPS, FRAMES, PLACES, D), 1.0, 6.0, ((0, 32), (1, 4)), (0, 3, 32, 2.75)),
    }


@jax.custom_vjp
def low(v):
    return lax.optimization_barrier(v.astype(jnp.bfloat16)).astype(jnp.float32)

@jax.custom_vjp
def low_back(v):
    return v

def low_keep(v):
    return (low(v), None)

def low_pass(kept, grad):
    return (grad,)

def back_keep(v):
    return (v, None)

def back_low(kept, grad):
    return (low(grad),)
low.defvjp(low_keep, low_pass)
low_back.defvjp(back_keep, back_low)
epsilon = 1e-06
SPATIAL = ('fqhe,fkhe->fhqk', 'fhqk,fkhe->fqhe')
TEMPORAL = ('fphe,gphe->phfg', 'phfg,gphe->fphe')

def normalize(stream, norm_gain, norm_shift):
    average = lax.optimization_barrier(jnp.mean(stream, axis=-1, keepdims=True))
    centred = stream - average
    variance = lax.optimization_barrier(jnp.mean(centred * centred, axis=-1, keepdims=True))
    return centred * lax.rsqrt(variance + epsilon) * norm_gain + norm_shift

def project(left, right):
    return jnp.einsum('fpd,dk->fpk', left, right, precision=lax.Precision.HIGHEST)

def attention_branch(stream, norm_gain, norm_shift, qkv_weight, qv_shift, out_weight, out_shift, forms):
    normed = low(normalize(stream, norm_gain, norm_shift))
    packed = project(normed, qkv_weight)
    head_shape = (FRAMES, PLACES, HEADS, HEAD_DIM)
    queries = low(low_back(packed[..., :D] + qv_shift[0])).reshape(head_shape)
    keys = low(low_back(packed[..., D:2 * D])).reshape(head_shape)
    values = low(low_back(packed[..., 2 * D:] + qv_shift[1])).reshape(head_shape)
    scores = jnp.einsum(forms[0], queries, keys, precision=lax.Precision.HIGHEST) * HEAD_DIM ** (-0.5)
    scores = low_back(scores)
    shares = low(jax.nn.softmax(scores, axis=-1))
    mixed = jnp.einsum(forms[1], shares, values, precision=lax.Precision.HIGHEST)
    mixed = low(low_back(mixed.reshape(FRAMES, PLACES, D)))
    branch_out = low_back(project(mixed, out_weight) + out_shift)
    return stream + branch_out

def mlp_branch(stream, norm_gain, norm_shift, up_weight, up_shift, down_weight, down_shift):
    normed = low(normalize(stream, norm_gain, norm_shift))
    before = low_back(project(normed, up_weight) + up_shift)
    hidden = low(jax.nn.gelu(before, approximate=False))
    return stream + low_back(project(hidden, down_weight) + down_shift)

def forward(stream, params):
    norm_gain, norm_bias, qkv_weight, qkv_bias, out_weight, out_bias, up_weight, up_bias, down_weight, down_bias = params
    for layer_index in range(LAYERS):
        stream = attention_branch(stream, norm_gain[layer_index, 0], norm_bias[layer_index, 0], qkv_weight[layer_index, 0], qkv_bias[layer_index, 0], out_weight[layer_index, 0], out_bias[layer_index, 0], SPATIAL)
        stream = attention_branch(stream, norm_gain[layer_index, 1], norm_bias[layer_index, 1], qkv_weight[layer_index, 1], qkv_bias[layer_index, 1], out_weight[layer_index, 1], out_bias[layer_index, 1], TEMPORAL)
        stream = mlp_branch(stream, norm_gain[layer_index, 2], norm_bias[layer_index, 2], up_weight[layer_index], up_bias[layer_index], down_weight[layer_index], down_bias[layer_index])
    return stream

def reference(clips, norm_gain, norm_bias, qkv_weight, qkv_bias, out_weight, out_bias, up_weight, up_bias, down_weight, down_bias, cotangent):
    params = tuple((member.astype(jnp.float32) for member in (norm_gain, norm_bias, qkv_weight, qkv_bias, out_weight, out_bias, up_weight, up_bias, down_weight, down_bias)))

    def one_clip(totals, inputs):
        clip_tokens, clip_cotangent = inputs
        result, pullback = jax.vjp(forward, clip_tokens.astype(jnp.float32), params)
        grad_input, grad_params = pullback(clip_cotangent.astype(jnp.float32))
        totals = jax.tree.map(jnp.add, totals, grad_params)
        return (totals, (result.astype(jnp.bfloat16), grad_input.astype(jnp.bfloat16)))
    zeros = tuple((jnp.zeros(member.shape, jnp.float32) for member in params))
    totals, outputs = lax.scan(one_clip, zeros, (clips, cotangent))
    return (outputs[0], outputs[1], totals[0], totals[1], totals[2], totals[3], totals[4], totals[5], totals[6], totals[7], totals[8], totals[9])
```

```python
import functools

import jax
import jax.numpy as jnp
from jax import lax
from jax.experimental import pallas as pl
from jax.experimental.pallas import tpu as pltpu
from jax.sharding import PartitionSpec as P

bf16, f32 = jnp.bfloat16, jnp.float32

MESH = pl.DeviceIdType.MESH
ORDERS = (("x","y","z"),("y","z","x"),("z","x","y"))
AXES = ("x","y","z")

def coords():
    f = lax.axis_index("fsdp"); s = lax.axis_index("seq")
    x = f // 8
    y = f % 4
    z = ((f // 4) % 2) * 2 + s // 2
    return {"x": x, "y": y, "z": z}, s % 2

def dev(at, c):
    return (at["x"] * 8 + (at["z"] // 2) * 4 + at["y"], (at["z"] % 2) * 2 + c)

def moved(at, axis, by):
    out = dict(at)
    out[axis] = (at[axis] + by + 4) % 4
    return out

def greet(at, c):
    bar = pltpu.get_barrier_semaphore()
    peers = [dev(moved(at, a, d), c) for a in AXES for d in (1, -1)] + [dev(at, 1 - c)]
    for p in peers:
        pl.semaphore_signal(bar, inc=1, device_id=p, device_id_type=MESH)
    pl.semaphore_wait(bar, len(peers))

def pick(g, b, c, p, sel, rows=None):
    def one(v):
        return pl.ds(0, 4) if v is None else pl.ds(*v) if isinstance(v, tuple) else v
    ref = g.at[b, c, p, one(sel["x"]), one(sel["z"]), one(sel["y"])]
    return ref if rows is None else ref.at[pl.ds(*rows), :]

class Gather:
    def __init__(self, s, g, b, p, at, c, sems):
        self.s, self.g, self.b, self.p, self.at, self.c = s, g, b, p, at, c
        self.ssem, self.rsem, self.lsem = sems
        self.order = ORDERS[p]
        self.pending = []
    def sel(self, stage, coord):
        out = {}
        for i, a in enumerate(self.order):
            out[a] = None if i < stage else (coord if i == stage else self.at[a])
        return out
    def half(self, stage, coord, h):
        out = self.sel(stage, coord); rows = None
        if stage == 0:
            rows = ((0, 32), (32, 16))[h]
        else:
            a = [a for a in self.order[:stage]]
            a = "x" if "x" in a else ("y" if "y" in a else "z")
            out[a] = (2 * h, 2)
        return out, rows
    def copy(self, k, sel, rows, to, src=None):
        d = pick(self.g, self.b, self.c, self.p, sel, rows)
        return pltpu.make_async_remote_copy(d if src is None else src, d, self.ssem.at[self.b, self.p, k], self.rsem.at[self.b, self.p, k], device_id=to, device_id_type=MESH)
    def go(self, *a, **k):
        cp = self.copy(*a, **k); cp.start(); self.pending.append(cp)
    def got(self, k, sel, rows):
        d = pick(self.g, self.b, self.c, self.p, sel, rows)
        pltpu.make_async_remote_copy(d, d, self.ssem.at[self.b, self.p, k], self.rsem.at[self.b, self.p, k], device_id=dev(self.at, 1 - self.c), device_id_type=MESH).wait_recv()
    def round(self, r):
        st, ph = divmod(r, 2)
        me, sib = self.c, dev(self.at, 1 - self.c)
        if 0 < r < 7:
            ps, pp = divmod(r - 1, 2)
            a = self.order[ps]; here = self.at[a]
            prev, nxt = (here + 3) % 4, (here + 1) % 4
            if pp == 0:
                self.got(ps * 4 + 0, self.sel(ps, prev), None)
                self.got(ps * 4 + 1, self.sel(ps, nxt), None)
            elif ps < 3:
                opp = (here + 2) % 4
                for h in (0, 1):
                    self.got(ps * 4 + 2 + h, *self.half(ps, opp, h))
        if st < 3:
            a = self.order[st]; here = self.at[a]
            prev, nxt = (here + 3) % 4, (here + 1) % 4
            up, down = dev(moved(self.at, a, 1), me), dev(moved(self.at, a, -1), me)
            if ph == 0:
                if r == 0:
                    own = self.s.at[self.b, self.c, self.p, self.at["z"] % 2]
                    d = pick(self.g, self.b, self.c, self.p, self.sel(0, here), None)
                    self.local = pltpu.make_async_copy(own, d, self.lsem.at[self.b, self.p])
                    self.local.start()
                if r == 2:
                    self.local.wait()
                sel = self.sel(st, here)
                if r == 0:
                    for k, to in ((0, up), (1, down)):
                        d = pick(self.g, self.b, self.c, self.p, sel, None)
                        cp = pltpu.make_async_remote_copy(own, d, self.ssem.at[self.b, self.p, k], self.rsem.at[self.b, self.p, k], device_id=to, device_id_type=MESH)
                        cp.start(); self.pending.append(cp)
                else:
                    self.go(st * 4 + 0, sel, None, up)
                    self.go(st * 4 + 1, sel, None, down)
                if st == 2:
                    self.go(12, sel, None, sib)
            else:
                self.go(st * 4 + 2, *self.half(st, prev, 0), up)
                self.go(st * 4 + 3, *self.half(st, nxt, 1), down)
                if st == 2:
                    self.go(13, self.sel(2, prev), None, sib)
                    self.go(14, self.sel(2, nxt), None, sib)
        elif r == 6:
            a = self.order[2]
            self.go(15, self.sel(2, (self.at[a] + 2) % 4), None, sib)
        elif r == 7:
            a = self.order[2]
            for k, by in ((12, 0), (13, 3), (14, 1), (15, 2)):
                d = pick(self.g, self.b, 1 - self.c, self.p, self.sel(2, (self.at[a] + by) % 4), None)
                pltpu.make_async_remote_copy(d, d, self.ssem.at[self.b, self.p, k], self.rsem.at[self.b, self.p, k], device_id=sib, device_id_type=MESH).wait_recv()
            for cp in self.pending: cp.wait_send()

class SmallGather:
    def __init__(self, s, gs, at, c, ssem, rsem, lsem):
        self.s, self.gs, self.at, self.c, self.ssem, self.rsem, self.lsem = s, gs, at, c, ssem, rsem, lsem
        self.sends = []
    def copy(self, ref, k, to, src=None):
        return pltpu.make_async_remote_copy(ref if src is None else src, ref, self.ssem.at[k], self.rsem.at[k], device_id=to, device_id_type=MESH)
    def send(self, *a, **k):
        cp = self.copy(*a, **k); cp.start(); self.sends.append(cp)
    def got(self, ref, k):
        self.copy(ref, k, dev(self.at, 1 - self.c)).wait_recv()
    def round(self, r):
        at, c, gs = self.at, self.c, self.gs
        x, y, z = at["x"], at["y"], at["z"]
        zh = z // 2
        nb = lambda a, d: dev(moved(at, a, d), c)
        blk = lambda by: gs.at[(x + by + 4) % 4, zh, y]
        row = lambda by: gs.at[:, zh, (y + by + 4) % 4]
        if r == 0:
            self.local = pltpu.make_async_copy(self.s, blk(0), self.lsem)
            self.local.start()
            self.send(blk(0), 0, nb("x", 1), src=self.s)
            self.send(blk(0), 1, nb("x", -1), src=self.s)
        if r == 1:
            self.got(blk(-1), 0)
            self.send(blk(-1), 2, nb("x", 1))
        if r == 2:
            self.got(blk(1), 1); self.got(blk(2), 2); self.local.wait()
            self.send(row(0), 3, nb("y", 1))
            self.send(row(0), 4, nb("y", -1))
        if r == 3:
            self.got(row(-1), 3)
            self.send(row(-1), 5, nb("y", 1))
        if r == 4:
            self.got(row(1), 4); self.got(row(2), 5)
            self.send(gs.at[:, zh], 6, dev({"x": x, "y": y, "z": 3 - z}, c))
        if r == 5:
            self.got(gs.at[:, 1 - zh], 6)
            for cp in self.sends: cp.wait_send()

def gather_kernel(nb, skew, s, ssm, g, gs, ssem, rsem, lsem, ss2, rs2, ls2):
    at, c = coords()
    greet(at, c)
    small = SmallGather(ssm, gs, at, c, ss2, rs2, ls2.at[0])
    parts = [[Gather(s, g, b, p, at, c, (ssem, rsem, lsem)) for p in range(3)] for b in range(nb)]
    for t in range(8 + skew * (nb - 1)):
        if t < 6: small.round(t)
        for b in range(nb):
            r = t - skew * b
            if 0 <= r < 8:
                for p in range(3): parts[b][p].round(r)

def gather(s, ssm, skew=1, cid=0):
    nb = s.shape[0]
    vm = pl.BlockSpec(memory_space=pltpu.VMEM)
    return pl.pallas_call(functools.partial(gather_kernel, nb, skew),
        out_shape=(jax.ShapeDtypeStruct((nb, 2, 3, 4, 4, 4, 48, 128), jnp.bfloat16), jax.ShapeDtypeStruct((4, 2, 4, 32, 128), jnp.bfloat16)),
        in_specs=[pl.BlockSpec(memory_space=pl.ANY), vm], out_specs=(pl.BlockSpec(memory_space=pl.ANY), vm),
        scratch_shapes=[pltpu.SemaphoreType.DMA((nb, 3, 16)), pltpu.SemaphoreType.DMA((nb, 3, 16)), pltpu.SemaphoreType.DMA((nb, 3)),
            pltpu.SemaphoreType.DMA((7,)), pltpu.SemaphoreType.DMA((7,)), pltpu.SemaphoreType.DMA((1,))],
        compiler_params=pltpu.CompilerParams(collective_id=cid, has_side_effects=True), name="gather")(s, ssm)

DIM = {"x": 0, "z": 1, "y": 2}

def at3(sel):
    out = []
    for a in ("x", "z", "y"):
        v = sel[a]
        out.append(pl.ds(0, 4) if v is None else pl.ds(*v) if isinstance(v, tuple) else v)
    return tuple(out)

class Reduce:
    def __init__(self, b, n, at, c, refs):
        self.b, self.at, self.c, self.slot = b, at, c, b % n
        (self.gr, self.red, self.A, self.B, self.R, self.ssem, self.rsem, self.lsem) = refs
        self.sib = dev(at, 1 - c)
        self.sends = []
    def order(self, p): return ORDERS[p][::-1]
    def nbr(self, p, st, by):
        return dev(moved(self.at, self.order(p)[st], by), self.c)
    def block(self, p, st, by, half=None):
        sel = {}
        for i, a in enumerate(self.order(p)):
            sel[a] = self.at[a] if i < st else (self.at[a] + by + 4) % 4 if i == st else None
        if half is not None and st < 2:
            rest = [a for a in ("x", "z", "y") if a in self.order(p)[st + 1:]]
            sel[rest[0]] = (2 * half, 2)
        ref = self.A.at[(self.b, p) + at3(sel)]
        if half is not None and st == 2:
            ref = ref.at[pl.ds(32 * half, 32 - 16 * half), :]
        return ref
    def land(self, p, st, k, half=None):
        ref = self.R[st].at[self.slot, p, k]
        if half is not None:
            ref = ref.at[pl.ds(2 * half, 2)] if st < 2 else ref.at[pl.ds(32 * half, 32 - 16 * half), :]
        return ref
    def copy(self, src, dst, p, k, to):
        return pltpu.make_async_remote_copy(src, dst, self.ssem.at[self.b, p, k], self.rsem.at[self.b, p, k], device_id=to, device_id_type=MESH)
    def send(self, *a):
        cp = self.copy(*a); cp.start(); self.sends.append(cp)
    def got(self, ref, p, k):
        self.copy(ref, ref, p, k, self.sib).wait_recv()
    def round(self, r):
        b, c, A = self.b, self.c, self.A
        if r == 0:
            self.local = pltpu.make_async_copy(self.gr.at[b, c], A.at[b], self.lsem.at[b])
            self.local.start()
            self.send(self.gr.at[b, 1 - c], self.B.at[self.slot], 0, 12, self.sib)
        if r == 1:
            self.local.wait()
            self.got(self.B.at[self.slot], 0, 12)
            @pl.loop(0, 12)
            def _(i):
                A[b, i // 4, i % 4] = A[b, i // 4, i % 4] + self.B[self.slot, i // 4, i % 4]
        if 2 <= r <= 7:
            st, ph = divmod(r - 2, 2)
            for p in range(3):
                if ph == 0:
                    for half, by in ((0, 1), (1, -1)):
                        dst, src = self.block(p, st, by, half), self.land(p, st, 2, half)
                        self.got(src, p, 4 * st + half)
                        dst[...] = dst[...] + src[...]
                    self.send(self.block(p, st, 1), self.land(p, st, 0), p, 4 * st + 2, self.nbr(p, st, 1))
                    self.send(self.block(p, st, -1), self.land(p, st, 1), p, 4 * st + 3, self.nbr(p, st, -1))
                else:
                    own = self.block(p, st, 0)
                    s0, s1 = self.land(p, st, 0), self.land(p, st, 1)
                    self.got(s0, p, 4 * st + 2)
                    self.got(s1, p, 4 * st + 3)
                    own[...] = (own[...].astype(f32) + s0[...].astype(f32) + s1[...].astype(f32)).astype(bf16)
        if r in (1, 3, 5):
            st = (r - 1) // 2
            for p in range(3):
                self.send(self.block(p, st, 2, 0), self.land(p, st, 2, 0), p, 4 * st + 0, self.nbr(p, st, 1))
                self.send(self.block(p, st, 2, 1), self.land(p, st, 2, 1), p, 4 * st + 1, self.nbr(p, st, -1))
        zl = self.at["z"] % 2
        if r == 7:
            own = A.at[b, :, self.at["x"], self.at["z"], self.at["y"]]
            mine = self.red.at[b, c, :, zl]
            self.local = pltpu.make_async_copy(own, mine, self.lsem.at[b])
            self.local.start()
            self.send(own, mine, 1, 12, dev(moved(self.at, "z", 1 - 2 * zl), c))
            self.send(own, mine, 2, 12, self.sib)
        if r == 8:
            other = self.red.at[b, c, :, 1 - zl]
            self.got(other, 1, 12)
            self.send(other, other, 0, 13, self.sib)
        if r == 9:
            self.local.wait()
            self.got(self.red.at[b, 1 - c, :, zl], 2, 12)
            self.got(self.red.at[b, 1 - c, :, 1 - zl], 0, 13)
            for cp in self.sends: cp.wait_send()

class Small:
    def __init__(self, at, c, sg, tot, bx, by, bz, ssem, rsem):
        self.at, self.c, self.sg, self.tot, self.bx, self.by, self.bz, self.ssem, self.rsem = at, c, sg, tot, bx, by, bz, ssem, rsem
        self.sends = []
    def copy(self, src, dst, k, to):
        return pltpu.make_async_remote_copy(src, dst, self.ssem.at[k], self.rsem.at[k], device_id=to, device_id_type=MESH)
    def send(self, *a):
        cp = self.copy(*a); cp.start(); self.sends.append(cp)
    def got(self, ref, k):
        self.copy(ref, ref, k, dev(self.at, 1 - self.c)).wait_recv()
    def round(self, r):
        at, c = self.at, self.c
        x, y, z = at["x"], at["y"], at["z"]
        zh, zl = z // 2, z % 2
        nb = lambda a, d: dev(moved(at, a, d), c)
        blk = lambda by: self.sg.at[(x + by + 4) % 4]
        row = lambda by: self.sg.at[x, :, (y + by + 4) % 4]
        def add(dst, *srcs):
            v = dst[...].astype(f32)
            for q in srcs: v = v + q[...].astype(f32)
            dst[...] = v.astype(bf16)
        if r == 0:
            self.send(blk(2), self.bx.at[0], 0, nb("x", 1))
            self.send(blk(-1), self.bx.at[1], 1, nb("x", -1))
        if r == 1:
            self.got(self.bx.at[0], 0)
            add(blk(1), self.bx.at[0])
            self.send(blk(1), self.bx.at[2], 2, nb("x", 1))
        if r == 2:
            self.got(self.bx.at[1], 1); self.got(self.bx.at[2], 2)
            add(blk(0), self.bx.at[1], self.bx.at[2])
            self.send(row(2), self.by.at[0], 3, nb("y", 1))
            self.send(row(-1), self.by.at[1], 4, nb("y", -1))
        if r == 3:
            self.got(self.by.at[0], 3)
            add(row(1), self.by.at[0])
            self.send(row(1), self.by.at[2], 5, nb("y", 1))
        if r == 4:
            self.got(self.by.at[1], 4); self.got(self.by.at[2], 5)
            add(row(0), self.by.at[1], self.by.at[2])
            self.send(self.sg.at[x, 1 - zh, y], self.bz.at[0], 6, dev({"x": x, "y": y, "z": 3 - z}, c))
        own = self.sg.at[x, zh, y]
        if r == 5:
            self.got(self.bz.at[0], 6)
            self.tot[0] = (own[...].astype(f32) + self.bz[0].astype(f32)).astype(bf16)
            self.send(self.tot.at[0], self.bz.at[1], 7, dev(moved(at, "z", 1 - 2 * zl), c))
        if r == 6:
            self.got(self.bz.at[1], 7)
            self.tot[1] = (self.tot[0].astype(f32) + self.bz[1].astype(f32)).astype(bf16)
            self.send(self.tot.at[1], self.bz.at[2], 8, dev(at, 1 - c))
        if r == 7:
            self.got(self.bz.at[2], 8)
            self.tot[2] = (self.tot[1].astype(f32) + self.bz[2].astype(f32)).astype(bf16)
            for cp in self.sends: cp.wait_send()

def reduce_kernel(nb, n, skew, gr, sgin, red, tot, A, B, R0, R1, R2, sg, bx, by, bz, ssem, rsem, lsem, ss2, rs2):
    at, c = coords()
    greet(at, c)
    sg[...] = sgin[...]
    small = Small(at, c, sg, tot, bx, by, bz, ss2, rs2)
    subs = [Reduce(b, n, at, c, (gr, red, A, B, (R0, R1, R2), ssem, rsem, lsem)) for b in range(nb)]
    for t in range(10 + skew * (nb - 1)):
        for b in range(nb):
            r = t - skew * b
            if 0 <= r < 10: subs[b].round(r)
        if t < 8: small.round(t)

def reduce(gr, sg, skew=1, n=3, cid=2):
    nb = gr.shape[0]
    V = lambda shape: pltpu.VMEM(shape, bf16)
    vm = pl.BlockSpec(memory_space=pltpu.VMEM)
    return pl.pallas_call(functools.partial(reduce_kernel, nb, n, skew),
        out_shape=(jax.ShapeDtypeStruct((nb, 2, 3, 2, 48, 128), bf16), jax.ShapeDtypeStruct((3, 32, 128), bf16)),
        in_specs=[pl.BlockSpec(memory_space=pl.ANY), vm], out_specs=(vm, vm),
        scratch_shapes=[V((nb, 3, 4, 4, 4, 48, 128)), V((n, 3, 4, 4, 4, 48, 128)), V((n, 3, 3, 4, 4, 48, 128)), V((n, 3, 3, 4, 48, 128)), V((n, 3, 3, 48, 128)),
            V((4, 2, 4, 32, 128)), V((3, 2, 4, 32, 128)), V((3, 2, 32, 128)), V((3, 32, 128)),
            pltpu.SemaphoreType.DMA((nb, 3, 14)), pltpu.SemaphoreType.DMA((nb, 3, 14)), pltpu.SemaphoreType.DMA((nb,)), pltpu.SemaphoreType.DMA((9,)), pltpu.SemaphoreType.DMA((9,))],
        compiler_params=pltpu.CompilerParams(collective_id=cid, has_side_effects=True, vmem_limit_bytes=63 << 20), name="reduce")(gr, sg)

T, D, F = 256, 768, 3072
NT = (((1,), (1,)), ((), ()))
NN = (((1,), (0,)), ((), ()))

def dot(a, b, dims=NN):
    return lax.dot_general(a, b, dims, preferred_element_type=f32)

def iota(shape, dim):
    return lax.broadcasted_iota(jnp.int32, shape, dim)

def chunk_at(m):
    return m // 6, (m // 2) % 3, m % 2

def stats(x):
    m = jnp.mean(x, axis=-1, keepdims=True)
    xc = x - m
    r = lax.rsqrt(jnp.mean(xc * xc, axis=-1, keepdims=True) + 1e-6)
    return xc * r, r

def norm_rows(u, gain, bias, a, step=32):
    @pl.loop(0, T, step=step)
    def _(i):
        at = pl.ds(i, step)
        n, _ = stats(u[at, :].astype(f32))
        a[at, :] = (n * gain + bias).astype(bf16)

def norm_back(u, gain, da, du, step=32):
    def body(i, carry):
        sg, sb = carry
        at = pl.ds(pl.multiple_of(i * step, step), step)
        n, r = stats(u[at, :].astype(f32))
        d = da[at, :]
        sg = sg + jnp.sum((d * n).reshape(step // 8, 8, D), axis=0)
        sb = sb + jnp.sum(d.reshape(step // 8, 8, D), axis=0)
        dn = d * gain
        c1 = jnp.mean(dn, axis=-1, keepdims=True)
        c2 = jnp.mean(dn * n, axis=-1, keepdims=True)
        du[at, :] = du[at, :] + r * (dn - c1 - n * c2)
        return sg, sb
    z = jnp.zeros((8, D), f32)
    sg, sb = lax.fori_loop(0, T // step, body, (z, z))
    return jnp.sum(sg, axis=0, keepdims=True), jnp.sum(sb, axis=0, keepdims=True)

def column_sum(x):
    return dot(jnp.ones((8, T), bf16), x)[0:1]

def attend(qkv, mask, o, lse_t, acc):
    lane = iota((1, 128), 1)
    acc[...] = jnp.zeros((T, 128), f32)
    @pl.loop(0, 6)
    def _(hp):
        off = pl.multiple_of(hp * 128, 128)
        q = qkv[:, pl.ds(off, 128)]
        k = qkv[:, pl.ds(off + D, 128)]
        v = qkv[:, pl.ds(off + 2 * D, 128)]
        mixed = None
        for h in range(2):
            mine = (lane // 64 == h)
            s = dot(q, k * jnp.where(mine, 0.125, 0.0).astype(bf16), NT) + mask[...]
            top = jnp.max(s, axis=-1, keepdims=True)
            e = jnp.exp(s - top)
            tot = jnp.sum(e, axis=-1, keepdims=True)
            p = (e * (1.0 / tot)).astype(bf16)
            part = dot(p, v * jnp.where(mine, 1.0, 0.0).astype(bf16))
            mixed = part if mixed is None else mixed + part
            acc[...] = jnp.where(lane == 2 * hp + h, top + jnp.log(tot), acc[...])
        o[:, pl.ds(off, 128)] = mixed.astype(bf16)
    lse_t[...] = acc[...].T[0:16, :]

def attend_back(qkv, mask, lse_t, do, delta_t, g, kt, dqt):
    lane = iota((1, 128), 1)
    kt[...] = (qkv[:, D:2 * D].astype(f32) * 0.125).T.astype(bf16)
    @pl.loop(0, 6)
    def _(hp):
        off = pl.multiple_of(hp * 128, 128)
        q = qkv[:, pl.ds(off, 128)]
        k = qkv[:, pl.ds(off + D, 128)]
        v = qkv[:, pl.ds(off + 2 * D, 128)]
        d = do[:, pl.ds(off, 128)]
        dk = dv = None
        for h in range(2):
            one = jnp.where(lane // 64 == h, 1.0, 0.0).astype(bf16)
            eighth = jnp.where(lane // 64 == h, 0.125, 0.0).astype(bf16)
            pt = jnp.exp(dot(k * eighth, q, NT) + mask[...] - lse_t[pl.ds(2 * hp + h, 1), :])
            dpt = dot(v * one, d, NT)
            dst = (pt * (dpt - delta_t[pl.ds(2 * hp + h, 1), :])).astype(bf16)
            a = dot(pt.astype(bf16), d * one)
            b = dot(dst, q * eighth)
            dv = a if dv is None else dv + a
            dk = b if dk is None else dk + b
            rows = pl.ds(pl.multiple_of(hp * 128 + h * 64, 64), 64)
            dqt[rows, :] = dot(kt[rows, :], dst)
        g[:, pl.ds(off + D, 128)] = dk.astype(bf16)
        g[:, pl.ds(off + 2 * D, 128)] = dv.astype(bf16)
    g[:, 0:D] = dqt[...].T.astype(bf16)

def head_sums(do, o, out):
    one = jnp.where(iota((16, D), 1) // 64 == iota((16, D), 0), 1.0, 0.0).astype(bf16)
    x = do[...].astype(f32) * o[...].astype(f32)
    hi = x.astype(bf16)
    lo = (x - hi.astype(f32)).astype(bf16)
    out[...] = dot(one, hi, NT) + dot(one, lo, NT)

class Vectors:
    @staticmethod
    def spread(gs, vec, upb):
        place = jnp.where((iota((128, D), 1) % 24 == iota((128, D), 0)), 1.0, 0.0).astype(bf16)
        own = iota((32, 1, D), 2) // 24 == iota((32, 1, D), 0)
        place4 = jnp.where((iota((128, F), 1) % 96 == iota((128, F), 0)), 1.0, 0.0).astype(bf16)
        own4 = iota((32, F), 1) // 96 == iota((32, F), 0)
        for l in range(2):
            x = gs[:, pl.ds(16 * l, 16), :]
            y = dot(x.reshape(512, 128), place).reshape(32, 16, D)
            vec[l] = jnp.sum(jnp.where(own, y, 0.0), axis=0)
            z = dot(x.astype(f32)[:, 13, :].astype(bf16), place4)
            upb[l] = jnp.sum(jnp.where(own4, z, 0.0), axis=0, keepdims=True)

    @staticmethod
    def collect(l, vecg, upg, sg):
        place = jnp.where((iota((D, 128), 0) % 24 == iota((D, 128), 1)), 1.0, 0.0).astype(bf16)
        own = iota((32, 1, D), 2) // 24 == iota((32, 1, D), 0)
        x = jnp.where(own, vecg[l][None], 0.0).astype(bf16).reshape(512, D)
        y = dot(x, place).reshape(32, 16, 128)
        place4 = jnp.where((iota((F, 128), 0) % 96 == iota((F, 128), 1)), 1.0, 0.0).astype(bf16)
        own4 = iota((32, F), 1) // 96 == iota((32, F), 0)
        z = dot(jnp.where(own4, upg[l], 0.0).astype(bf16), place4)
        y = jnp.where(iota((32, 16, 128), 1) == 13, z[:, None, :], y)
        sg[:, pl.ds(16 * l, 16), :] = y.astype(bf16)

def unpack_chunk(st, w, lo, hi):
    @pl.loop(0, 16, unroll=4)
    def _(i):
        x = st[pl.ds(2 * i, 2)].astype(f32).reshape(2, 2, 24, 128)
        at = pl.ds(pl.multiple_of(48 * i, 48), 48)
        w[at, pl.ds(lo, 128)] = x[:, 0].reshape(48, 128).astype(bf16)
        w[at, pl.ds(hi, 128)] = x[:, 1].reshape(48, 128).astype(bf16)

def pack_pair(r):
    a = r[:, :128].reshape(32, 24, 128)
    b = r[:, 128:].reshape(32, 24, 128)
    return jnp.concatenate([a, b], axis=1).astype(bf16).reshape(4, 2, 4, 48, 128)

def compute_kernel(gw, gs, clips, cot, out, dclips, gr, sg,
                   wqkv, wo, wup, wdn, stage, stg, su, sqkv, so, slse, su2, sh, sgp,
                   vec, upb, vecg, upg, masks, a_buf, t_buf, ht, e_buf, do_buf, g_buf, dz_buf, da, du, dqt, acc, delta, x3f, x3p, rp, rf,
                   wsem, gsem, tss, trs, tls):
    s = lax.axis_index("seq")
    bar = pltpu.get_barrier_semaphore()
    fs = lax.axis_index("fsdp")
    for i in range(1, 4):
        pl.semaphore_signal(bar, inc=1, device_id=(fs, (s + i) % 4), device_id_type=MESH)
    pl.semaphore_wait(bar, 3)

    def exchange(n, src, dst, to_places):
        cps = []
        for i in range(4):
            t = (s + i) % 4
            if to_places:
                a, b = src.at[:, pl.ds(pl.multiple_of(t * 16, 16), 16), :], dst.at[pl.ds(4 * s, 4)]
            else:
                a, b = src.at[pl.ds(4 * t, 4)], dst.at[:, pl.ds(pl.multiple_of(s * 16, 16), 16), :]
            if i == 0:
                cp = pltpu.make_async_copy(a, b, tls.at[n])
            else:
                cp = pltpu.make_async_remote_copy(a, b, tss.at[n, i - 1], trs.at[n, i - 1], device_id=(fs, t), device_id_type=MESH)
            cp.start()
            cps.append(cp)
        return cps
    def finish(cps):
        for cp in cps: cp.wait()

    first = exchange(0, cot, rp.at[0], True)
    Vectors.spread(gs, vec, upb)
    r0, r1 = iota((T, T), 0), iota((T, T), 1)
    masks[0] = jnp.where(r0 // 64 == r1 // 64, 0.0, -1e30)
    masks[1] = jnp.where(r0 % 16 == r1 % 16, 0.0, -1e30)

    def load(l):
        def fetch(n):
            j, m = divmod(n, 12)
            c, p, zl = chunk_at(m)
            return pltpu.make_async_copy(gw.at[4 * l + j, c, p, :, :, zl], stage.at[n % 4], wsem.at[n % 4])
        downs = []
        for m in range(12):
            c, p, zl = chunk_at(m)
            cp = pltpu.make_async_copy(gw.at[4 * l + 3, c, p, :, :, zl], wdn.at[:, :, :, m % 2, :, pl.ds(128 * (m // 2), 128)], wsem.at[4 + m])
            cp.start(); downs.append(cp)
        for n in range(3): fetch(n).start()
        for n in range(36):
            if n + 3 < 36: fetch(n + 3).start()
            fetch(n).wait()
            j, m = divmod(n, 12)
            st = stage.at[n % 4].reshape(32, 48, 128)
            if j < 2:
                if m < 9: unpack_chunk(st, wqkv.at[j], 128 * m, 1152 + 128 * m)
                else: unpack_chunk(st, wo.at[j], 128 * (m - 9), 384 + 128 * (m - 9))
            else: unpack_chunk(st, wup, 128 * m, 1536 + 128 * m)
        for cp in downs: cp.wait()

    def branch(l, k, put):
        u = su.at[l, k]
        v = vec.at[l]
        norm_rows(u, v[k:k + 1], v[3 + k:4 + k], a_buf)
        @pl.loop(0, 9)
        def _(n):
            off = pl.multiple_of(n * 256, 256)
            y = dot(a_buf[...], wqkv[k, :, pl.ds(off, 256)])
            third = off // D
            within = pl.multiple_of(off - third * D, 256)
            bias = jnp.where(third == 0, v[pl.ds(6 + 2 * k, 1), pl.ds(within, 256)], jnp.where(third == 2, v[pl.ds(7 + 2 * k, 1), pl.ds(within, 256)], 0.0))
            sqkv[l, k, :, pl.ds(off, 256)] = (y + bias).astype(bf16)
        attend(sqkv.at[l, k], masks.at[k], so.at[l, k], slse.at[l, k], acc)
        for n in range(3):
            at = slice(256 * n, 256 * n + 256)
            put(at, u[:, at].astype(f32) + dot(so[l, k], wo[k, :, at]) + v[10 + k:11 + k, at])

    def forward(l):
        def put1(at, y): x3f[l, :, :, at] = y.astype(bf16).reshape(4, 64, 256)
        branch(l, 0, put1)
        finish(exchange(1 + 2 * l, x3f.at[l], rp.at[1 + l], True))
        su[l, 1] = rp[1 + l].reshape(T, D)
        def put2(at, y): su2[l, :, at] = y
        branch(l, 1, put2)
        v = vec.at[l]
        norm_rows(su2.at[l], v[2:3], v[5:6], a_buf)
        @pl.loop(0, 12)
        def _(n):
            at = pl.ds(pl.multiple_of(n * 256, 256), 256)
            z = dot(a_buf[...], wup[:, at]) + upb[l, :, at]
            cdf = 0.5 * (1.0 + lax.erf(z * 0.7071067811865476))
            sh[l, :, at] = (z * cdf).astype(bf16)
            sgp[l, :, at] = (cdf + z * (0.3989422804014327 * jnp.exp(-0.5 * z * z))).astype(bf16)
        for n in range(3):
            at = slice(256 * n, 256 * n + 256)
            y = su2[l, :, at] + dot(sh[l], wdn[:, :, :, :, :, at].reshape(F, 256)) + v[12:13, at]
            x3p[l, :, :, at] = y.astype(bf16).reshape(16, 16, 256)
        return exchange(2 + 2 * l, x3p.at[l], rf.at[0] if l == 0 else out, False)

    def flush(l, j):
        cps = []
        cp = pltpu.make_async_copy(stg.at[j % 2], gr.at[4 * l + j], gsem.at[j % 2])
        cp.start()
        return cp

    def branch_back(l, k):
        u, v = su.at[l, k], vec.at[l]
        e_buf[...] = du[...].astype(bf16)
        t_buf[...] = so[l, k].T
        slot = k % 2
        for i in range(3):
            c, p, zl = chunk_at(9 + i)
            pair = jnp.concatenate([e_buf[:, 128 * i:128 * i + 128], e_buf[:, 384 + 128 * i:512 + 128 * i]], axis=1)
            stg[slot, c, p, :, :, zl] = pack_pair(dot(t_buf[...], pair))
        vecg[l, 10 + k:11 + k, :] = column_sum(e_buf[...])
        for n in range(3):
            at = slice(256 * n, 256 * n + 256)
            do_buf[:, at] = dot(e_buf[...], wo[k, at, :], NT).astype(bf16)
        head_sums(do_buf, so.at[l, k], delta)
        attend_back(sqkv.at[l, k], masks.at[k], slse.at[l, k], do_buf, delta, g_buf, t_buf, dqt)
        vecg[l, 6 + 2 * k:7 + 2 * k, :] = column_sum(g_buf[:, 0:D])
        vecg[l, 7 + 2 * k:8 + 2 * k, :] = column_sum(g_buf[:, 2 * D:3 * D])
        norm_rows(u, v[k:k + 1], v[3 + k:4 + k], a_buf)
        t_buf[...] = a_buf[...].T
        @pl.loop(0, 9)
        def _(m):
            c, p, zl = chunk_at(m)
            lo = pl.multiple_of(128 * m, 128)
            pair = jnp.concatenate([g_buf[:, pl.ds(lo, 128)], g_buf[:, pl.ds(1152 + lo, 128)]], axis=1)
            stg[slot, c, p, :, :, zl] = pack_pair(dot(t_buf[...], pair))
        cp = flush(l, k)
        for n in range(3):
            at = slice(256 * n, 256 * n + 256)
            da[:, at] = dot(g_buf[...], wqkv[k, at, :], NT)
        dg, db = norm_back(u, v[k:k + 1], da, du)
        vecg[l, k:k + 1, :] = dg
        vecg[l, 3 + k:4 + k, :] = db
        return cp

    def mlp_back(l):
        v = vec.at[l]
        e_buf[...] = du[...].astype(bf16)
        ht[...] = sh[l].T
        for i in range(4):
            for n in range(3):
                r = dot(ht[768 * i:768 * i + 768, :], e_buf[:, 256 * n:256 * n + 256]).astype(bf16).reshape(2, 4, 2, 48, 256)
                for q in range(2):
                    for hh in range(2):
                        c, p, zl = chunk_at(2 * (2 * n + q) + hh)
                        stg[1, c, p, i, :, zl] = r[:, :, hh, :, 128 * q:128 * q + 128]
        c3 = flush(l, 3)
        vecg[l, 12:13, :] = column_sum(e_buf[...])
        for i in range(8):
            at = slice(384 * i, 384 * i + 384)
            w = wdn[i // 2, i % 2].reshape(384, D)
            dz_buf[:, at] = (dot(e_buf[...], w, NT) * sgp[l, :, at].astype(f32)).astype(bf16)
        upg[l] = column_sum(dz_buf[...])
        norm_rows(su2.at[l], v[2:3], v[5:6], a_buf)
        t_buf[...] = a_buf[...].T
        @pl.loop(0, 12)
        def _(m):
            c, p, zl = chunk_at(m)
            lo = pl.multiple_of(128 * m, 128)
            pair = jnp.concatenate([dz_buf[:, pl.ds(lo, 128)], dz_buf[:, pl.ds(1536 + lo, 128)]], axis=1)
            stg[0, c, p, :, :, zl] = pack_pair(dot(t_buf[...], pair))
        c2 = flush(l, 2)
        for n in range(3):
            at = slice(256 * n, 256 * n + 256)
            da[:, at] = dot(dz_buf[...], wup[at, :], NT)
        dg, db = norm_back(su2.at[l], v[2:3], da, du)
        vecg[l, 2:3, :] = dg
        vecg[l, 5:6, :] = db
        return c3, c2

    su[0, 0] = clips[...].reshape(T, D)
    load(0)
    finish(forward(0))
    su[1, 0] = rf[0].reshape(T, D)
    load(1)
    last = forward(1)
    finish(first)
    du[...] = rp[0].reshape(T, D).astype(f32)
    vecg[...] = jnp.zeros_like(vecg)
    for l in (1, 0):
        c3, c2 = mlp_back(l)
        c3.wait()
        c1 = branch_back(l, 1)
        x3p[2 + l] = du[...].astype(bf16).reshape(16, 16, D)
        cps = exchange(6 - l, x3p.at[2 + l], rf.at[1 + l], False)
        c2.wait()
        finish(cps)
        du[...] = rf[1 + l].reshape(T, D).astype(f32)
        c0 = branch_back(l, 0)
        if l == 1:
            x3f[2] = du[...].astype(bf16).reshape(4, 64, D)
            cps = exchange(7, x3f.at[2], rp.at[3], True)
            finish(last)
            load(0)
            finish(cps)
            du[...] = rp[3].reshape(T, D).astype(f32)
        c1.wait(); c0.wait()
        Vectors.collect(l, vecg, upg, sg)
    dclips[...] = du[...].astype(bf16).reshape(4, 64, D)

def compute(gw, gs, clips, cot, cid=1):
    V = lambda shape, dt: pltpu.VMEM(shape, dt)
    vm = pl.BlockSpec(memory_space=pltpu.VMEM)
    anys = pl.BlockSpec(memory_space=pl.ANY)
    scratch = [
        V((2, D, 3 * D), bf16), V((2, D, D), bf16), V((D, F), bf16), V((4, 2, 4, 2, 48, D), bf16),
        V((4, 4, 2, 4, 48, 128), bf16), V((2, 2, 3, 4, 2, 2, 4, 48, 128), bf16),
        V((2, 2, T, D), bf16), V((2, 2, T, 3 * D), bf16), V((2, 2, T, D), bf16), V((2, 2, 16, T), f32),
        V((2, T, D), f32), V((2, T, F), bf16), V((2, T, F), bf16),
        V((2, 16, D), f32), V((2, 1, F), f32), V((2, 16, D), f32), V((2, 1, F), f32), V((2, T, T), f32),
        V((T, D), bf16), V((D, T), bf16), V((F, T), bf16), V((T, D), bf16), V((T, D), bf16), V((T, 3 * D), bf16), V((T, F), bf16),
        V((T, D), f32), V((T, D), f32), V((D, T), f32), V((T, 128), f32), V((16, T), f32),
        V((3, 4, 64, D), bf16), V((4, 16, 16, D), bf16), V((4, 16, 16, D), bf16), V((3, 4, 64, D), bf16),
        pltpu.SemaphoreType.DMA((16,)), pltpu.SemaphoreType.DMA((2,)), pltpu.SemaphoreType.DMA((8, 3)), pltpu.SemaphoreType.DMA((8, 3)), pltpu.SemaphoreType.DMA((8,)),
    ]
    return pl.pallas_call(compute_kernel,
        out_shape=(jax.ShapeDtypeStruct((4, 64, D), bf16), jax.ShapeDtypeStruct((4, 64, D), bf16),
                   jax.ShapeDtypeStruct((8, 2, 3, 4, 2, 2, 4, 48, 128), bf16), jax.ShapeDtypeStruct((32, 32, 128), bf16)),
        in_specs=[anys, vm, vm, vm], out_specs=(vm, vm, anys, vm),
        scratch_shapes=scratch,
        compiler_params=pltpu.CompilerParams(collective_id=cid, has_side_effects=True, vmem_limit_bytes=63 << 20), name="compute")(gw, gs, clips, cot)

D = 768

def pack_weights(qkv, out, up, down):
    q = qkv.reshape(2, 2, 24, 2, 9, 128).transpose(0, 1, 4, 3, 2, 5).reshape(2, 2, 9, 48, 128)
    o = out.reshape(2, 2, 24, 2, 3, 128).transpose(0, 1, 4, 3, 2, 5).reshape(2, 2, 3, 48, 128)
    u = up.reshape(2, 24, 2, 12, 128).transpose(0, 3, 2, 1, 4).reshape(2, 1, 12, 48, 128)
    d = down.reshape(2, 2, 48, 6, 128).transpose(0, 3, 1, 2, 4).reshape(2, 1, 12, 48, 128)
    a = jnp.concatenate([q, o], axis=2)
    return jnp.concatenate([a, u, d], axis=1).reshape(8, 2, 3, 2, 48, 128)

def unpack_weights(red):
    r = red.reshape(2, 4, 12, 48, 128).astype(f32)
    q = r[:, :2, :9].reshape(2, 2, 9, 2, 24, 128).transpose(0, 1, 4, 3, 2, 5).reshape(2, 2, 24, 2304)
    o = r[:, :2, 9:].reshape(2, 2, 3, 2, 24, 128).transpose(0, 1, 4, 3, 2, 5).reshape(2, 2, 24, 768)
    u = r[:, 2].reshape(2, 12, 2, 24, 128).transpose(0, 3, 2, 1, 4).reshape(2, 24, 3072)
    d = r[:, 3].reshape(2, 6, 2, 48, 128).transpose(0, 2, 3, 1, 4).reshape(2, 96, 768)
    return q, o, u, d

def pack_small(gain, bias, qb, ob, ub, db):
    rows = jnp.concatenate([gain, bias, qb.reshape(2, 4, 24), ob, db[:, None]], axis=1)
    rows = jnp.pad(rows, ((0, 0), (0, 0), (0, 104)))
    last = jnp.pad(ub, ((0, 0), (0, 32)))[:, None]
    return jnp.concatenate([rows, last, jnp.zeros((2, 2, 128), bf16)], axis=1).reshape(32, 128)

def unpack_small(tot):
    t = tot.reshape(2, 16, 128).astype(f32)
    v = t[:, :13, :24]
    return v[:, 0:3], v[:, 3:6], v[:, 6:10].reshape(2, 2, 2, 24), v[:, 10:12], t[:, 13, :96], v[:, 12]

def local(clips, gain, bias, qkv, qb, out, ob, up, ub, down, db, cot):
    gw, gs = gather(pack_weights(qkv, out, up, down), pack_small(gain, bias, qb, ob, ub, db))
    y, dx, gr, sg = compute(gw.reshape(8, 2, 3, 4, 2, 2, 4, 48, 128), gs.reshape(32, 32, 128), clips[0], cot[0])
    r, tot = reduce(gr.reshape(8, 2, 3, 4, 4, 4, 48, 128), sg.reshape(4, 2, 4, 32, 128))
    gq, go, gu, gd = unpack_weights(r)
    gg, gb, gqb, gob, gub, gdb = unpack_small(tot[2])
    return y[None], dx[None], gg, gb, gq, gqb, go, gob, gu, gub, gd, gdb

def solution(mesh):
    f = P("fsdp", "seq", None, None)
    ins = (f, P(None, None, "fsdp"), P(None, None, "fsdp"), P(None, None, "fsdp", None), P(None, None, None, "fsdp"), P(None, None, "fsdp", None),
        P(None, None, "fsdp"), P(None, "fsdp", None), P(None, "fsdp"), P(None, "fsdp", None), P(None, "fsdp"), f)
    return jax.shard_map(local, mesh=mesh, in_specs=ins, out_specs=(f, f) + ins[1:11], check_vma=False)
```

```python
import functools
import jax
import jax.numpy as jnp
from jax import lax
from jax.experimental import pallas as pl
from jax.experimental.pallas import tpu as pltpu
from jax.sharding import PartitionSpec as P
MESH = pl.DeviceIdType.MESH
bf16, f32 = jnp.bfloat16, jnp.float32
T, D, F = 256, 768, 3072
NN = (((1,), (0,)), ((), ()))
NT = (((1,), (1,)), ((), ()))
ORDERS = (("x", "y", "z"), ("y", "z", "x"), ("z", "x", "y"))
STORED = ("x", "z", "y")

def coords():
    f, s = lax.axis_index("fsdp"), lax.axis_index("seq")
    return {"x": f // 8, "y": f % 4, "z": ((f // 4) % 2) * 2 + s // 2}, s % 2

def dev(at, c):
    return (at["x"] * 8 + (at["z"] // 2) * 4 + at["y"], (at["z"] % 2) * 2 + c)

def moved(at, axis, by):
    return {**at, axis: (at[axis] + by + 4) % 4}

def greet(at, c):
    bar = pltpu.get_barrier_semaphore()
    other = moved(at, "z", 1 - 2 * (at["z"] % 2))
    peers = [dev(moved(at, a, d), c) for a in "xyz" for d in (1, -1)] + [dev(at, 1 - c), dev(other, 1 - c)]
    for p in peers:
        pl.semaphore_signal(bar, inc=1, device_id=p, device_id_type=MESH)
    pl.semaphore_wait(bar, len(peers))

def remote(src, dst, ssem, rsem, to):
    return pltpu.make_async_remote_copy(src, dst, ssem, rsem, device_id=to, device_id_type=MESH)

def index(sel):
    return tuple(pl.ds(0, 4) if v is None else pl.ds(*v) if isinstance(v, tuple) else v for v in sel)

class Gather:
    ROUNDS = 8
    def __init__(self, s, g, b, p, at, c, sems):
        self.s, self.g, self.b, self.p, self.at, self.c = s, g, b, p, at, c
        self.ssem, self.rsem, self.lsem = sems
        self.order, self.pending = ORDERS[p], []
    def ref(self, st, coord, half=None, c=None):
        sel = {}
        for i, a in enumerate(self.order):
            sel[a] = None if i < st else coord if i == st else self.at[a]
        if half is not None and st > 0:
            sel[[a for a in STORED if a in self.order[:st]][0]] = (2 * half, 2)
        ref = self.g.at[(self.b, self.c if c is None else c, self.p) + index(sel[a] for a in STORED)]
        return ref if half is None or st > 0 else ref.at[pl.ds(32 * half, 32 - 16 * half), :]
    def copy(self, src, dst, k, to):
        return remote(src, dst, self.ssem.at[self.b, self.p, k], self.rsem.at[self.b, self.p, k], to)
    def go(self, ref, k, to, src=None):
        cp = self.copy(ref if src is None else src, ref, k, to)
        cp.start()
        self.pending.append(cp)
    def got(self, ref, k):
        self.copy(ref, ref, k, dev(self.at, 1 - self.c)).wait_recv()
    def round(self, r):
        sib = dev(self.at, 1 - self.c)
        last = self.at[self.order[2]]
        if 0 < r < 7:
            st, ph = divmod(r - 1, 2)
            here = self.at[self.order[st]]
            if ph == 0:
                self.got(self.ref(st, (here + 3) % 4), 4 * st)
                self.got(self.ref(st, (here + 1) % 4), 4 * st + 1)
            else:
                for h in (0, 1):
                    self.got(self.ref(st, (here + 2) % 4, h), 4 * st + 2 + h)
        if r < 6:
            st, ph = divmod(r, 2)
            a = self.order[st]
            here = self.at[a]
            up, down = (dev(moved(self.at, a, d), self.c) for d in (1, -1))
            own = self.ref(st, here)
            if ph == 0:
                src = None
                if r == 0:
                    src = self.s.at[self.b, self.c, self.p, self.at["z"] % 2]
                    self.local = pltpu.make_async_copy(src, own, self.lsem.at[self.b, self.p])
                    self.local.start()
                if r == 2:
                    self.local.wait()
                self.go(own, 4 * st, up, src)
                self.go(own, 4 * st + 1, down, src)
                if st == 2:
                    self.go(own, 12, sib)
            else:
                self.go(self.ref(st, (here + 3) % 4, 0), 4 * st + 2, up)
                self.go(self.ref(st, (here + 1) % 4, 1), 4 * st + 3, down)
                if st == 2:
                    self.go(self.ref(2, (here + 3) % 4), 13, sib)
                    self.go(self.ref(2, (here + 1) % 4), 14, sib)
        if r == 6:
            self.go(self.ref(2, (last + 2) % 4), 15, sib)
        if r == 7:
            for k, by in ((12, 0), (13, 3), (14, 1), (15, 2)):
                self.got(self.ref(2, (last + by) % 4, c=1 - self.c), k)
    def end(self):
        for cp in self.pending:
            cp.wait_send()

class Point:
    def __init__(self, at, c, ssem, rsem):
        self.at, self.c, self.ssem, self.rsem, self.sends = at, c, ssem, rsem, []
    def send(self, src, dst, k, to):
        cp = remote(src, dst, self.ssem.at[k], self.rsem.at[k], to)
        cp.start()
        self.sends.append(cp)
    def got(self, ref, k):
        remote(ref, ref, self.ssem.at[k], self.rsem.at[k], dev(self.at, 1 - self.c)).wait_recv()
    def near(self, a, d):
        return dev(moved(self.at, a, d), self.c)
    def end(self):
        for cp in self.sends:
            cp.wait_send()

class SmallGather(Point):
    def __init__(self, s, gs, at, c, ssem, rsem, lsem):
        super().__init__(at, c, ssem, rsem)
        self.s, self.gs, self.lsem = s, gs, lsem
    def round(self, r):
        at, gs = self.at, self.gs
        x, y, zh = at["x"], at["y"], at["z"] // 2
        blk = lambda by: gs.at[(x + by + 4) % 4, zh, y]
        row = lambda by: gs.at[:, zh, (y + by + 4) % 4]
        if r == 0:
            self.local = pltpu.make_async_copy(self.s, blk(0), self.lsem)
            self.local.start()
            self.send(self.s, blk(0), 0, self.near("x", 1))
            self.send(self.s, blk(0), 1, self.near("x", -1))
        if r == 1:
            self.got(blk(-1), 0)
            self.send(blk(-1), blk(-1), 2, self.near("x", 1))
        if r == 2:
            self.got(blk(1), 1)
            self.got(blk(2), 2)
            self.local.wait()
            self.send(row(0), row(0), 3, self.near("y", 1))
            self.send(row(0), row(0), 4, self.near("y", -1))
        if r == 3:
            self.got(row(-1), 3)
            self.send(row(-1), row(-1), 5, self.near("y", 1))
        if r == 4:
            self.got(row(1), 4)
            self.got(row(2), 5)
            self.send(gs.at[:, zh], gs.at[:, zh], 6, dev({**at, "z": 3 - at["z"]}, self.c))
        if r == 5:
            self.got(gs.at[:, 1 - zh], 6)

class Reduce:
    ROUNDS = 10
    def __init__(self, n, b, at, c, gr, red, held, land, sums, sems):
        self.n, self.b, self.at, self.c = n, b, at, c
        self.gr, self.red, self.held, self.land, self.sums = gr, red, held, land, sums
        self.ssem, self.rsem, self.lsem = sems
        self.sib = dev(at, 1 - c)
        self.pending = {}
    def block(self, p, st, by, half=None):
        order = ORDERS[p][::-1]
        sel = {a: None for a in STORED if a not in order[:st]}
        sel[order[st]] = (self.at[order[st]] + by + 4) % 4
        if half is not None and st < 2:
            sel[[a for a in sel if a != order[st]][0]] = (2 * half, 2)
        ref = self.sums[st].at[(self.n % self.sums[st].shape[0], p) + index(sel.values())]
        return ref.at[pl.ds(32 * half, 32 - 16 * half), :] if half is not None and st == 2 else ref
    def arrival(self, p, st, k, half=None):
        ref = self.land[st].at[self.n % self.land[st].shape[0], p, k]
        if half is None:
            return ref
        return ref.at[pl.ds(2 * half, 2)] if st < 2 else ref.at[pl.ds(32 * half, 32 - 16 * half), :]
    def copy(self, src, dst, p, k, to):
        return remote(src, dst, self.ssem.at[self.b, p, k], self.rsem.at[self.b, p, k], to)
    def send(self, group, *a):
        cp = self.copy(*a)
        cp.start()
        self.pending.setdefault(group, []).append(cp)
    def got(self, ref, p, k):
        self.copy(ref, ref, p, k, self.sib).wait_recv()
    def sent(self, group):
        for cp in self.pending.pop(group, []):
            cp.wait_send()
    def near(self, p, st, by):
        return dev(moved(self.at, ORDERS[p][2 - st], by), self.c)
    def halves(self, st):
        for p in range(3):
            self.send(st, self.block(p, st, 2, 0), self.arrival(p, st, 2, 0), p, 4 * st + 0, self.near(p, st, 1))
            self.send(st, self.block(p, st, 2, 1), self.arrival(p, st, 2, 1), p, 4 * st + 1, self.near(p, st, -1))
    def round(self, r):
        b, c = self.b, self.c
        zl = self.at["z"] % 2
        a = self.n % self.sums[0].shape[0]
        if r == 0:
            self.local = pltpu.make_async_copy(self.gr.at[b, c], self.sums[0].at[a], self.lsem.at[b])
            self.local.start()
            self.send("sib", self.gr.at[b, 1 - c], self.held.at[self.n % self.held.shape[0]], 0, 12, self.sib)
        if r == 1:
            held = self.held.at[self.n % self.held.shape[0]]
            self.local.wait()
            self.got(held, 0, 12)
            mine = self.sums[0].at[a]
            for p in range(3):
                for x in range(4):
                    mine[p, x] = mine[p, x] + held[p, x]
            self.halves(0)
        if 2 <= r <= 7:
            st, ph = divmod(r - 2, 2)
            for p in range(3):
                if ph == 0:
                    for half, by in ((0, 1), (1, -1)):
                        dst, src = self.block(p, st, by, half), self.arrival(p, st, 2, half)
                        self.got(src, p, 4 * st + half)
                        dst[...] = dst[...] + src[...]
                    self.send(st, self.block(p, st, 1), self.arrival(p, st, 0), p, 4 * st + 2, self.near(p, st, 1))
                    self.send(st, self.block(p, st, -1), self.arrival(p, st, 1), p, 4 * st + 3, self.near(p, st, -1))
                else:
                    s0, s1 = self.arrival(p, st, 0), self.arrival(p, st, 1)
                    self.got(s0, p, 4 * st + 2)
                    self.got(s1, p, 4 * st + 3)
                    total = self.block(p, st, 0)[...].astype(f32) + s0[...].astype(f32) + s1[...].astype(f32)
                    self.sums[st + 1][self.n % self.sums[st + 1].shape[0], p] = total.astype(bf16)
            if r in (3, 5):
                self.halves(st + 1)
        if r == 7:
            own, mine = self.sums[3].at[self.n % self.sums[3].shape[0]], self.red.at[b, c, :, zl]
            self.local = pltpu.make_async_copy(own, mine, self.lsem.at[b])
            self.local.start()
            self.send(3, own, mine, 1, 12, dev(moved(self.at, "z", 1 - 2 * zl), c))
            self.send(3, own, mine, 2, 12, self.sib)
        if r == 8:
            other = self.red.at[b, c, :, 1 - zl]
            self.got(other, 1, 12)
            self.send("end", other, other, 0, 13, self.sib)
        if r == 9:
            self.local.wait()
            self.got(self.red.at[b, 1 - c, :, zl], 2, 12)
            self.got(self.red.at[b, 1 - c, :, 1 - zl], 0, 13)
    def end(self):
        for g in list(self.pending):
            self.sent(g)

class SmallReduce(Point):
    def __init__(self, sg, tot, bx, by, bz, at, c, ssem, rsem):
        super().__init__(at, c, ssem, rsem)
        self.sg, self.tot, self.bx, self.by, self.bz = sg, tot, bx, by, bz
    def round(self, r):
        at, sg, tot, bx, by, bz = self.at, self.sg, self.tot, self.bx, self.by, self.bz
        x, y, z = at["x"], at["y"], at["z"]
        zh, zl = z // 2, z % 2
        blk = lambda d: sg.at[(x + d + 4) % 4]
        row = lambda d: sg.at[x, :, (y + d + 4) % 4]
        def add(dst, *more):
            v = dst[...].astype(f32)
            for q in more:
                v = v + q[...].astype(f32)
            dst[...] = v.astype(bf16)
        if r == 0:
            self.send(blk(2), bx.at[0], 0, self.near("x", 1))
            self.send(blk(-1), bx.at[1], 1, self.near("x", -1))
        if r == 1:
            self.got(bx.at[0], 0)
            add(blk(1), bx.at[0])
            self.send(blk(1), bx.at[2], 2, self.near("x", 1))
        if r == 2:
            self.got(bx.at[1], 1)
            self.got(bx.at[2], 2)
            add(blk(0), bx.at[1], bx.at[2])
            self.send(row(2), by.at[0], 3, self.near("y", 1))
            self.send(row(-1), by.at[1], 4, self.near("y", -1))
        if r == 3:
            self.got(by.at[0], 3)
            add(row(1), by.at[0])
            self.send(row(1), by.at[2], 5, self.near("y", 1))
        if r == 4:
            self.got(by.at[1], 4)
            self.got(by.at[2], 5)
            add(row(0), by.at[1], by.at[2])
            self.send(sg.at[x, 1 - zh, y], bz.at[0], 6, dev({**at, "z": 3 - z}, self.c))
        if r == 5:
            self.got(bz.at[0], 6)
            tot[0] = (sg[x, zh, y].astype(f32) + bz[0].astype(f32)).astype(bf16)
            self.send(tot.at[0], bz.at[1], 7, self.near("z", 1 - 2 * zl))
        if r == 6:
            self.got(bz.at[1], 7)
            tot[1] = (tot[0].astype(f32) + bz[1].astype(f32)).astype(bf16)
            self.send(tot.at[1], bz.at[2], 8, dev(at, 1 - self.c))
        if r == 7:
            self.got(bz.at[2], 8)
            tot[2] = (tot[1].astype(f32) + bz[2].astype(f32)).astype(bf16)

def exchange(n, src, dst, to_places, sems):
    f, s = lax.axis_index("fsdp"), lax.axis_index("seq")
    ssem, rsem, lsem = sems
    cps = []
    for i in (2, 3, 1, 0):
        t = (s + i) % 4
        if to_places:
            a, b = src.at[:, pl.ds(pl.multiple_of(t * 16, 16), 16), :], dst.at[pl.ds(4 * s, 4)]
        else:
            a, b = src.at[pl.ds(4 * t, 4)], dst.at[:, pl.ds(pl.multiple_of(s * 16, 16), 16), :]
        cp = pltpu.make_async_copy(a, b, lsem.at[n]) if i == 0 else remote(a, b, ssem.at[n, i - 1], rsem.at[n, i - 1], (f, t))
        cp.start()
        cps.append(cp)
    return cps

def finish(cps):
    for cp in cps:
        cp.wait()

def dot(a, b, dims=NN):
    return lax.dot_general(a, b, dims, preferred_element_type=f32)

def iota(shape, dim):
    return lax.broadcasted_iota(jnp.int32, shape, dim)

def chunk_at(m):
    return m // 6, (m // 2) % 3, m % 2

def cols(n, w=256):
    return slice(w * n, w * n + w)

def stats(x):
    xc = x - jnp.mean(x, axis=-1, keepdims=True)
    r = lax.rsqrt(jnp.mean(xc * xc, axis=-1, keepdims=True) + 1e-6)
    return xc * r, r

def norm_rows(u, gain, bias, a):
    for i in range(8):
        at = cols(i, 32)
        n, _ = stats(u[at, :].astype(f32))
        a[at, :] = (n * gain + bias).astype(bf16)

def norm_back(u, gain, da, du):
    sg = sb = jnp.zeros((8, D), f32)
    for i in range(8):
        at = cols(i, 32)
        n, r = stats(u[at, :].astype(f32))
        d = da[at, :]
        sg = sg + jnp.sum((d * n).reshape(4, 8, D), axis=0)
        sb = sb + jnp.sum(d.reshape(4, 8, D), axis=0)
        dn = d * gain
        c1 = jnp.mean(dn, axis=-1, keepdims=True)
        c2 = jnp.mean(dn * n, axis=-1, keepdims=True)
        du[at, :] = du[at, :] + r * (dn - c1 - n * c2)
    return jnp.sum(sg, axis=0, keepdims=True), jnp.sum(sb, axis=0, keepdims=True)

def column_sum(x):
    return dot(jnp.ones((8, T), bf16), x)[0:1]

def lanes(h, value):
    return jnp.where(iota((1, 128), 1) // 64 == h, value, 0.0).astype(bf16)

def attend(qkv, mask, o, lse_t, acc):
    lane = iota((1, 128), 1)
    for hp in range(6):
        q, k, v = (qkv[:, cols(6 * i + hp, 128)] for i in range(3))
        mixed = None
        for h in range(2):
            s = dot(q, k * lanes(h, 0.125), NT) + mask[...]
            top = jnp.max(s, axis=-1, keepdims=True)
            e = jnp.exp(s - top)
            tot = jnp.sum(e, axis=-1, keepdims=True)
            part = dot((e * (1.0 / tot)).astype(bf16), v * lanes(h, 1.0))
            mixed = part if mixed is None else mixed + part
            lse = top + jnp.log(tot)
            acc[...] = jnp.where(lane == 2 * hp + h, lse, 0.0 if hp + h == 0 else acc[...])
        o[:, cols(hp, 128)] = mixed.astype(bf16)
    lse_t[...] = acc[...].T[0:16, :]

def attend_back(qkv, mask, lse_t, do, delta_t, g, kt, dqt):
    kt[...] = (qkv[:, D:2 * D].astype(f32) * 0.125).T.astype(bf16)
    for hp in range(6):
        q, k, v = (qkv[:, cols(6 * i + hp, 128)] for i in range(3))
        d = do[:, cols(hp, 128)]
        dk = dv = None
        for h in range(2):
            row = slice(2 * hp + h, 2 * hp + h + 1)
            pt = jnp.exp(dot(k * lanes(h, 0.125), q, NT) + mask[...] - lse_t[row, :])
            dpt = dot(v * lanes(h, 1.0), d, NT)
            dst = (pt * (dpt - delta_t[row, :])).astype(bf16)
            a = dot(pt.astype(bf16), d * lanes(h, 1.0))
            b = dot(dst, q * lanes(h, 0.125))
            dv = a if dv is None else dv + a
            dk = b if dk is None else dk + b
            rows = cols(2 * hp + h, 64)
            dqt[rows, :] = dot(kt[rows, :], dst)
        g[:, cols(6 + hp, 128)] = dk.astype(bf16)
        g[:, cols(12 + hp, 128)] = dv.astype(bf16)
    g[:, 0:D] = dqt[...].T.astype(bf16)

def head_sums(do, o, out):
    one = jnp.where(iota((16, D), 1) // 64 == iota((16, D), 0), 1.0, 0.0).astype(bf16)
    x = do[...].astype(f32) * o[...].astype(f32)
    hi = x.astype(bf16)
    lo = (x - hi.astype(f32)).astype(bf16)
    out[...] = dot(one, hi, NT) + dot(one, lo, NT)

def set_masks(masks):
    r0, r1 = iota((T, T), 0), iota((T, T), 1)
    masks[0] = jnp.where(r0 // 64 == r1 // 64, 0.0, -1e30)
    masks[1] = jnp.where(r0 % 16 == r1 % 16, 0.0, -1e30)

def spread(gs, vec, upb):
    place = jnp.where((iota((128, D), 1) % 24 == iota((128, D), 0)), 1.0, 0.0).astype(bf16)
    own = iota((32, 1, D), 2) // 24 == iota((32, 1, D), 0)
    place4 = jnp.where((iota((128, F), 1) % 96 == iota((128, F), 0)), 1.0, 0.0).astype(bf16)
    own4 = iota((32, F), 1) // 96 == iota((32, F), 0)
    for l in range(2):
        x = gs[:, :, :, pl.ds(16 * l, 16), :].reshape(32, 16, 128)
        y = dot(x.reshape(512, 128), place).reshape(32, 16, D)
        vec[l] = jnp.sum(jnp.where(own, y, 0.0), axis=0)
        z = dot(x.astype(f32)[:, 13, :].astype(bf16), place4)
        upb[l] = jnp.sum(jnp.where(own4, z, 0.0), axis=0, keepdims=True)

def collect(l, vecg, upg, sg):
    place = jnp.where((iota((D, 128), 0) % 24 == iota((D, 128), 1)), 1.0, 0.0).astype(bf16)
    own = iota((32, 1, D), 2) // 24 == iota((32, 1, D), 0)
    x = jnp.where(own, vecg[l][None], 0.0).astype(bf16).reshape(512, D)
    y = dot(x, place).reshape(32, 16, 128)
    place4 = jnp.where((iota((F, 128), 0) % 96 == iota((F, 128), 1)), 1.0, 0.0).astype(bf16)
    own4 = iota((32, F), 1) // 96 == iota((32, F), 0)
    z = dot(jnp.where(own4, upg[l], 0.0).astype(bf16), place4)
    y = jnp.where(iota((32, 16, 128), 1) == 13, z[:, None, :], y)
    sg[:, :, :, pl.ds(16 * l, 16), :] = y.astype(bf16).reshape(4, 2, 4, 16, 128)

def unpack_chunk(st, w, lo, hi):
    for i in range(16):
        x = st[pl.ds(2 * i, 2)].astype(f32).reshape(2, 2, 24, 128)
        at = cols(i, 48)
        w[at, pl.ds(lo, 128)] = x[:, 0].reshape(48, 128).astype(bf16)
        w[at, pl.ds(hi, 128)] = x[:, 1].reshape(48, 128).astype(bf16)

def pack_pair(r):
    a, b = r[:, :128].reshape(32, 24, 128), r[:, 128:].reshape(32, 24, 128)
    return jnp.concatenate([a, b], axis=1).astype(bf16).reshape(4, 2, 4, 48, 128)

def pair(x, lo, hi):
    return jnp.concatenate([x[:, lo:lo + 128], x[:, hi:hi + 128]], axis=1)


OFFS = (0, 2, 4, 6, 8, 10, 12, 14)

def forward_kernel(s, ss, clips, cot, gw, wqkv_o, wo_o, wup_o, wdn_o, qkv_o, o_o, lse_o, u_o, u2_o, h_o, gp_o, vec_o, cot_o, y_o,
                   gs, wqkv, wo, wup, wdn, stage, su, sqkv, so, slse, su2, sh, sgp, vec, upb, masks, a_buf, acc, x3f, x3p, rp, rf, y3,
                   gss, grs, gls, sss, srs, sls, ess, ers, els, wsem, osem):
    at, c = coords()
    greet(at, c)
    small = SmallGather(ss, gs, at, c, sss, srs, sls.at[0])
    parts = [[Gather(s, gw, b, p, at, c, (gss, grs, gls)) for p in range(3)] for b in range(8)]
    state = {"t": 0, "out": 0}
    ready, fetched, unpacked, done = set(), {}, set(), set()
    esems = (ess, ers, els)
    saves = {}

    def save(key, src, dst):
        cp = pltpu.make_async_copy(src, dst, osem.at[state["out"]])
        state["out"] += 1
        cp.start()
        saves[key] = cp

    def fetch(b):
        l, j = divmod(b, 4)
        gz = gw.reshape(8, 2, 3, 4, 2, 2, 4, 48, 128)
        cps = []
        if j == 3 and l:
            saves.pop((0, 3)).wait()
        for m in range(12):
            ci, p, zl = chunk_at(m)
            dst = stage.at[b % 2, m] if j < 3 else wdn.at[:, :, :, m % 2, :, pl.ds(128 * (m // 2), 128)]
            cp = pltpu.make_async_copy(gz.at[b, ci, p, :, :, zl], dst, wsem.at[b % 2, m])
            cp.start()
            cps.append(cp)
        fetched[b] = cps

    def try_fetch():
        for b in range(8):
            if b in ready and b not in fetched and (b < 2 or b - 2 in unpacked) and (b % 4 < 3 or b < 4 or b - 4 in done):
                fetch(b)

    def slot():
        t = state["t"]
        if t > OFFS[-1] + 7:
            return
        if t < 6:
            small.round(t)
        for b in reversed(range(8)):
            r = t - OFFS[b]
            if 0 <= r < 8:
                for p in range(3):
                    parts[b][p].round(r)
                if r == 7:
                    ready.add(b)
        state["t"] += 1
        try_fetch()

    def poll(b):
        if b < 7 and state["t"] <= OFFS[b + 1] + 7:
            slot()

    def weights(b):
        l, j = divmod(b, 4)
        while b not in ready:
            slot()
        try_fetch()
        cps = fetched[b]
        if j < 3 and l:
            saves.pop((0, j)).wait()
            if j < 2:
                saves.pop((0, j, 0)).wait()
        for m in range(12):
            cps[m].wait()
            if j == 3:
                continue
            st = stage.at[b % 2, m].reshape(32, 48, 128)
            if j == 2:
                unpack_chunk(st, wup, 128 * m, 1536 + 128 * m)
            elif m < 9:
                unpack_chunk(st, wqkv.at[j], 128 * m, 1152 + 128 * m)
            else:
                unpack_chunk(st, wo.at[j], 128 * (m - 9), 384 + 128 * (m - 9))
        unpacked.add(b)
        if j < 2:
            save((l, j), wqkv.at[j], wqkv_o.at[l, j])
            save((l, j, 0), wo.at[j], wo_o.at[l, j])
        else:
            save((l, j), *((wup, wup_o.at[l]) if j == 2 else (wdn, wdn_o.at[l])))
        try_fetch()

    def branch(l, k, put):
        b = 4 * l + k
        weights(b)
        u, v = su.at[l, k], vec.at[l]
        norm_rows(u, v[k:k + 1], v[3 + k:4 + k], a_buf)
        save(("u", l, k), u, u_o.at[l, k])
        for n in range(9):
            y = dot(a_buf[...], wqkv[k, :, cols(n)])
            if n // 3 != 1:
                y = y + v[6 + 2 * k + n // 6:7 + 2 * k + n // 6, cols(n % 3)]
            sqkv[l, k, :, cols(n)] = y.astype(bf16)
        save(("q", l, k), sqkv.at[l, k], qkv_o.at[l, k])
        poll(b)
        attend(sqkv.at[l, k], masks.at[k], so.at[l, k], slse.at[l, k], acc)
        save(("o", l, k), so.at[l, k], o_o.at[l, k])
        for n in range(3):
            put(n, u[:, cols(n)].astype(f32) + dot(so[l, k], wo[k, :, cols(n)]) + v[10 + k:11 + k, cols(n)])
        done.add(b)

    def layer(l):
        def put1(n, y):
            x3f[l, :, :, cols(n)] = y.astype(bf16).reshape(4, 64, 256)
        branch(l, 0, put1)
        cps = exchange(1 + 2 * l, x3f.at[l], rp.at[1 + l], True, esems)
        poll(4 * l)
        finish(cps)
        su[l, 1] = rp[1 + l].reshape(T, D)
        def put2(n, y):
            su2[l, :, cols(n)] = y
        branch(l, 1, put2)
        save(("u2", l), su2.at[l], u2_o.at[l])
        poll(4 * l + 1)
        weights(4 * l + 2)
        v = vec.at[l]
        norm_rows(su2.at[l], v[2:3], v[5:6], a_buf)
        for n in range(12):
            z = dot(a_buf[...], wup[:, cols(n)]) + upb[l, :, cols(n)]
            cdf = 0.5 * (1.0 + lax.erf(z * 0.7071067811865476))
            sh[l, :, cols(n)] = (z * cdf).astype(bf16)
            sgp[l, :, cols(n)] = (cdf + z * (0.3989422804014327 * jnp.exp(-0.5 * z * z))).astype(bf16)
            if n == 5:
                poll(4 * l + 2)
        save(("h", l), sh.at[l], h_o.at[l])
        save(("gp", l), sgp.at[l], gp_o.at[l])
        done.add(4 * l + 2)
        poll(4 * l + 2)
        weights(4 * l + 3)
        out = x3p if l == 0 else y3
        for n in range(3):
            y = su2[l, :, cols(n)] + dot(sh[l], wdn[:, :, :, :, :, cols(n)].reshape(F, 256)) + v[12:13, cols(n)]
            out[:, :, cols(n)] = y.astype(bf16).reshape(16, 16, 256)
        done.add(4 * l + 3)
        if l == 0:
            cps = exchange(2, x3p, rf, False, esems)
            poll(3)
            finish(cps)
            su[1, 0] = rf[...].reshape(T, D)
        else:
            save("y", y3, y_o)
            save("lse", slse, lse_o)

    slot()
    first = exchange(0, cot, rp.at[0], True, esems)
    set_masks(masks)
    su[0, 0] = clips[...].reshape(T, D)
    for _ in range(5):
        slot()
    spread(gs, vec, upb)
    save("vec", vec, vec_o)
    layer(0)
    finish(first)
    save("cot", rp.at[0], cot_o)
    layer(1)
    for ps in parts:
        for g in ps:
            g.end()
    small.end()
    for cp in saves.values():
        cp.wait()

def forward(s, ss, clips, cot, cid=0):
    V = pltpu.VMEM
    S = lambda *shape: pltpu.SemaphoreType.DMA(shape)
    vm, hbm = pl.BlockSpec(memory_space=pltpu.VMEM), pl.BlockSpec(memory_space=pl.ANY)
    o = lambda *shape, dt=bf16: jax.ShapeDtypeStruct(shape, dt)
    outs = (o(8, 2, 3, 4, 4, 4, 48, 128), o(2, 2, D, 3 * D), o(2, 2, D, D), o(2, D, F), o(2, 4, 2, 4, 2, 48, D),
            o(2, 2, T, 3 * D), o(2, 2, T, D), o(2, 2, 16, T, dt=f32), o(2, 2, T, D), o(2, T, D, dt=f32), o(2, T, F), o(2, T, F),
            o(2, 16, D, dt=f32), o(16, 16, D), o(16, 16, D))
    scratch = [
        V((4, 2, 4, 32, 128), bf16), V((2, D, 3 * D), bf16), V((2, D, D), bf16), V((D, F), bf16), V((4, 2, 4, 2, 48, D), bf16),
        V((2, 12, 4, 2, 4, 48, 128), bf16), V((2, 2, T, D), bf16), V((2, 2, T, 3 * D), bf16), V((2, 2, T, D), bf16), V((2, 2, 16, T), f32),
        V((2, T, D), f32), V((2, T, F), bf16), V((2, T, F), bf16), V((2, 16, D), f32), V((2, 1, F), f32), V((2, T, T), f32),
        V((T, D), bf16), V((T, 128), f32), V((2, 4, 64, D), bf16), V((16, 16, D), bf16), V((3, 16, 16, D), bf16), V((4, 64, D), bf16), V((16, 16, D), bf16),
        S(8, 3, 16), S(8, 3, 16), S(8, 3), S(7), S(7), S(1), S(4, 3), S(4, 3), S(4), S(2, 12), S(40)]
    return pl.pallas_call(forward_kernel, out_shape=outs, in_specs=[vm] * 4, out_specs=tuple([hbm] * 15), scratch_shapes=scratch,
        compiler_params=pltpu.CompilerParams(collective_id=cid, has_side_effects=True, vmem_limit_bytes=63 << 20), name="forward")(s, ss, clips, cot)


SKEW = 2
OLD_FIRST = True

def backward_kernel(wqkv_i, wo_i, wup_i, wdn_i, qkv_i, o_i, lse_i, u_i, u2_i, h_i, gp_i, vec, cot_i, y_i, out, dclips, gr, red, tot,
                    wqkv, wo, wup, wdn, sqkv, so, slse, su, su2, sh, sgp, masks, a_buf, t_buf, e_buf, do_buf, g_buf, da, du, dqt, delta,
                    vecg, upg, gstage, y3, x3p, x3f, rf, rp, held, l0, l1, l2, s0, s1, s2, s3, sg, bx, by, bz,
                    rss, rrs, rls, sss, srs, ess, ers, els, isem, gsem):
    at, c = coords()
    greet(at, c)
    esems = (ess, ers, els)
    grz, grc = gr.reshape(8, 2, 3, 4, 2, 2, 4, 48, 128), gr
    subs = [Reduce(n, 7 - n, at, c, grc, red, held, (l0, l1, l2), (s0, s1, s2, s3), (rss, rrs, rls)) for n in range(8)]
    small = SmallReduce(sg, tot, bx, by, bz, at, c, sss, srs)
    state = {"t": 0, "made": 0, "in": 0}
    loads = {}

    def slot():
        t = state["t"]
        if t > SKEW * 7 + 9:
            return
        order = range(8) if OLD_FIRST else reversed(range(8))
        for n in order:
            r = t - SKEW * n
            if 0 <= r < 10:
                if r == 0 and n >= 2: subs[n - 2].sent(0)
                if r in (3, 5, 7) and n >= 2: subs[n - 2].sent((r - 1) // 2)
                subs[n].round(r)
        state["t"] += 1

    def poll():
        if state["t"] < SKEW * state["made"]:
            slot()

    def load(key, src, dst):
        cp = pltpu.make_async_copy(src, dst, isem.at[state["in"]])
        state["in"] += 1
        cp.start()
        loads.setdefault(key, []).append(cp)

    def have(key):
        for cp in loads.pop(key, []):
            cp.wait()

    def load_mlp(l):
        load((l, "dn"), wdn_i.at[l], wdn)
        load((l, "gp"), gp_i.at[l], sgp)
        load((l, "h"), h_i.at[l], sh)
        load((l, "up"), wup_i.at[l], wup)
        load((l, "u2"), u2_i.at[l], su2)

    def load_branch(l, k):
        load((l, k, "w"), wo_i.at[l, k], wo.at[k])
        load((l, k, "q"), qkv_i.at[l, k], sqkv.at[k])
        load((l, k, "q"), o_i.at[l, k], so.at[k])
        load((l, k, "w"), wqkv_i.at[l, k], wqkv.at[k])
        load((l, k, "q"), u_i.at[l, k], su.at[k])

    flushes = {}

    def flush(b, m, q):
        ci, p, zl = chunk_at(m)
        cp = pltpu.make_async_copy(gstage.at[q], grz.at[b, ci, p, :, :, zl], gsem.at[q])
        cp.start()
        flushes[q] = cp

    def room(q):
        if q in flushes:
            flushes.pop(q).wait()

    def made(b):
        for q in list(flushes):
            room(q)
        state["made"] += 1

    def weight_grads(b, first, todo):
        for m, left, right in todo:
            q = m % 8
            room(q)
            gstage[q] = pack_pair(dot(left[...], right()))
            flush(b, m, q)

    def mlp(l):
        v = vec.at[l]
        e = e_buf.at[2]
        e[...] = du[...].astype(bf16)
        have((l, "dn"))
        have((l, "gp"))
        for i in range(8):
            w = wdn[i // 2, i % 2].reshape(384, D)
            sgp[:, cols(i, 384)] = (dot(e[...], w, NT) * sgp[:, cols(i, 384)].astype(f32)).astype(bf16)
        have((l, "up"))
        for n in range(3):
            da[:, cols(n)] = dot(sgp[...], wup[cols(n), :], NT)
        have((l, "u2"))
        dg, db = norm_back(su2, v[2:3], da, du)
        vecg[l, 2:3, :] = dg
        vecg[l, 5:6, :] = db

    def mlp_down_grads(l):
        e = e_buf.at[2]
        have((l, "h"))
        for n in range(3):
            for q in range(4): room(4 * (n % 2) + q)
            for i in range(4):
                t = sh[:, cols(i, 768)].T
                r = dot(t, e[:, cols(n)]).astype(bf16).reshape(2, 4, 2, 48, 256)
                for q in range(2):
                    for hh in range(2):
                        gstage[4 * (n % 2) + 2 * q + hh, i] = r[:, :, hh, :, cols(q, 128)]
            for q in range(4): flush(4 * l + 3, 4 * n + q, 4 * (n % 2) + q)
        vecg[l, 12:13, :] = column_sum(e[...])
        made(4 * l + 3)

    def mlp_up_grads(l):
        v = vec.at[l]
        norm_rows(su2, v[2:3], v[5:6], a_buf)
        t_buf[...] = a_buf[...].T
        weight_grads(4 * l + 2, 0, [(m, t_buf, functools.partial(pair, sgp, 128 * m, 1536 + 128 * m)) for m in range(12)])
        upg[l] = column_sum(sgp[...])
        made(4 * l + 2)

    def branch(l, k, midway):
        v = vec.at[l]
        e = e_buf.at[k]
        e[...] = du[...].astype(bf16)
        have((l, k, "w"))
        have((l, k, "q"))
        for n in range(3):
            do_buf[:, cols(n)] = dot(e[...], wo[k, cols(n), :], NT).astype(bf16)
        head_sums(do_buf, so.at[k], delta)
        midway()
        attend_back(sqkv.at[k], masks.at[k], slse.at[l, k], do_buf, delta, g_buf, t_buf, dqt)
        midway()
        for n in range(3):
            da[:, cols(n)] = dot(g_buf[...], wqkv[k, cols(n), :], NT)
        dg, db = norm_back(su.at[k], v[k:k + 1], da, du)
        vecg[l, k:k + 1, :] = dg
        vecg[l, 3 + k:4 + k, :] = db

    def branch_grads(l, k):
        v = vec.at[l]
        e = e_buf.at[k]
        t_buf[...] = so[k].T
        weight_grads(4 * l + k, 9, [(9 + i, t_buf, functools.partial(pair, e, 128 * i, 384 + 128 * i)) for i in range(3)])
        norm_rows(su.at[k], v[k:k + 1], v[3 + k:4 + k], a_buf)
        t_buf[...] = a_buf[...].T
        weight_grads(4 * l + k, 0, [(m, t_buf, functools.partial(pair, g_buf, 128 * m, 1152 + 128 * m)) for m in range(9)])
        vecg[l, 10 + k:11 + k, :] = column_sum(e[...])
        vecg[l, 6 + 2 * k:7 + 2 * k, :] = column_sum(g_buf[:, 0:D])
        vecg[l, 7 + 2 * k:8 + 2 * k, :] = column_sum(g_buf[:, 2 * D:3 * D])
        made(4 * l + k)

    load(("du",), cot_i, rp)
    load_mlp(1)
    load(("lse",), lse_i, slse)
    load_branch(1, 1)
    load(("y",), y_i, y3)
    load_branch(1, 0)
    set_masks(masks)
    vecg[...] = jnp.zeros_like(vecg)
    have(("du",))
    du[...] = rp[...].reshape(T, D).astype(f32)
    have(("lse",))
    for l in (1, 0):
        mlp(l)
        if l == 1:
            have(("y",))
            last = exchange(0, y3, out, False, esems)
        mlp_down_grads(l)
        poll()
        mlp_up_grads(l)
        if l == 1:
            load_mlp(0)
        poll()
        branch(l, 1, poll)
        x3p[...] = du[...].astype(bf16).reshape(16, 16, D)
        cps = exchange(1 + l, x3p, rf.at[l], False, esems)
        branch_grads(l, 1)
        if l == 1:
            load_branch(0, 1)
        poll()
        finish(cps)
        du[...] = rf[l].reshape(T, D).astype(f32)
        branch(l, 0, poll)
        if l == 1:
            x3f[...] = du[...].astype(bf16).reshape(4, 64, D)
            cps = exchange(3, x3f, rp, True, esems)
        branch_grads(l, 0)
        if l == 1:
            load_branch(0, 0)
            poll()
            finish(cps)
            du[...] = rp[...].reshape(T, D).astype(f32)
        collect(l, vecg, upg, sg)
    dclips[...] = du[...].astype(bf16).reshape(4, 64, D)
    finish(last)
    r = 0
    while state["t"] <= SKEW * 7 + 9:
        slot()
        if r < 8:
            small.round(r)
            r += 1
    while r < 8:
        small.round(r)
        r += 1
    for s in subs:
        s.end()
    small.end()

def backward(wqkv, wo, wup, wdn, qkv, o, lse, u, u2, h, gp, vec, cot, y, cid=1):
    V = pltpu.VMEM
    S = lambda *shape: pltpu.SemaphoreType.DMA(shape)
    vm, hbm = pl.BlockSpec(memory_space=pltpu.VMEM), pl.BlockSpec(memory_space=pl.ANY)
    sd = lambda *shape, dt=bf16: jax.ShapeDtypeStruct(shape, dt)
    outs = (sd(4, 64, D), sd(4, 64, D), sd(8, 2, 3, 4, 4, 4, 48, 128), sd(8, 2, 3, 2, 48, 128), sd(3, 32, 128))
    scratch = [
        V((2, D, 3 * D), bf16), V((2, D, D), bf16), V((D, F), bf16), V((4, 2, 4, 2, 48, D), bf16),
        V((2, T, 3 * D), bf16), V((2, T, D), bf16), V((2, 2, 16, T), f32), V((2, T, D), bf16), V((T, D), f32), V((T, F), bf16), V((T, F), bf16),
        V((2, T, T), f32), V((T, D), bf16), V((D, T), bf16), V((3, T, D), bf16), V((T, D), bf16), V((T, 3 * D), bf16), V((T, D), f32), V((T, D), f32), V((D, T), f32), V((16, T), f32),
        V((2, 16, D), f32), V((2, 1, F), f32), V((8, 4, 2, 4, 48, 128), bf16), V((16, 16, D), bf16), V((16, 16, D), bf16), V((4, 64, D), bf16), V((2, 4, 64, D), bf16), V((16, 16, D), bf16),
        V((2, 3, 4, 4, 4, 48, 128), bf16), V((2, 3, 3, 4, 4, 48, 128), bf16), V((2, 3, 3, 4, 48, 128), bf16), V((2, 3, 3, 48, 128), bf16),
        V((2, 3, 4, 4, 4, 48, 128), bf16), V((2, 3, 4, 4, 48, 128), bf16), V((2, 3, 4, 48, 128), bf16), V((2, 3, 48, 128), bf16),
        V((4, 2, 4, 32, 128), bf16), V((3, 2, 4, 32, 128), bf16), V((3, 2, 32, 128), bf16), V((3, 32, 128), bf16),
        S(8, 3, 14), S(8, 3, 14), S(8), S(9), S(9), S(4, 3), S(4, 3), S(4), S(40), S(8)]
    return pl.pallas_call(backward_kernel, out_shape=outs, in_specs=[hbm] * 11 + [vm] + [hbm] * 2, out_specs=(vm, vm, hbm, vm, vm), scratch_shapes=scratch,
        compiler_params=pltpu.CompilerParams(collective_id=cid, has_side_effects=True, vmem_limit_bytes=63 << 20), name="backward")(
            wqkv, wo, wup, wdn, qkv, o, lse, u, u2, h, gp, vec, cot, y)


def pack_weights(qkv, out, up, down):
    q = qkv.reshape(2, 2, 24, 2, 9, 128).transpose(0, 1, 4, 3, 2, 5).reshape(2, 2, 9, 48, 128)
    o = out.reshape(2, 2, 24, 2, 3, 128).transpose(0, 1, 4, 3, 2, 5).reshape(2, 2, 3, 48, 128)
    u = up.reshape(2, 24, 2, 12, 128).transpose(0, 3, 2, 1, 4).reshape(2, 1, 12, 48, 128)
    d = down.reshape(2, 2, 48, 6, 128).transpose(0, 3, 1, 2, 4).reshape(2, 1, 12, 48, 128)
    a = jnp.concatenate([q, o], axis=2)
    return jnp.concatenate([a, u, d], axis=1).reshape(8, 2, 3, 2, 48, 128)

def unpack_weights(red):
    r = red.reshape(2, 4, 12, 48, 128).astype(f32)
    q = r[:, :2, :9].reshape(2, 2, 9, 2, 24, 128).transpose(0, 1, 4, 3, 2, 5).reshape(2, 2, 24, 2304)
    o = r[:, :2, 9:].reshape(2, 2, 3, 2, 24, 128).transpose(0, 1, 4, 3, 2, 5).reshape(2, 2, 24, 768)
    u = r[:, 2].reshape(2, 12, 2, 24, 128).transpose(0, 3, 2, 1, 4).reshape(2, 24, 3072)
    d = r[:, 3].reshape(2, 6, 2, 48, 128).transpose(0, 2, 3, 1, 4).reshape(2, 96, 768)
    return q, o, u, d

def pack_small(gain, bias, qb, ob, ub, db):
    rows = jnp.concatenate([gain, bias, qb.reshape(2, 4, 24), ob, db[:, None]], axis=1)
    rows = jnp.pad(rows, ((0, 0), (0, 0), (0, 104)))
    last = jnp.pad(ub, ((0, 0), (0, 32)))[:, None]
    return jnp.concatenate([rows, last, jnp.zeros((2, 2, 128), bf16)], axis=1).reshape(32, 128)

def unpack_small(tot):
    t = tot.reshape(2, 16, 128).astype(f32)
    v = t[:, :13, :24]
    return v[:, 0:3], v[:, 3:6], v[:, 6:10].reshape(2, 2, 2, 24), v[:, 10:12], t[:, 13, :96], v[:, 12]

def local(clips, gain, bias, qkv, qb, out, ob, up, ub, down, db, cot):
    g, *saved = forward(pack_weights(qkv, out, up, down), pack_small(gain, bias, qb, ob, ub, db), clips[0], cot[0])
    y, dx, _, r, tot = backward(*saved)
    gq, go, gu, gd = unpack_weights(r)
    gg, gb, gqb, gob, gub, gdb = unpack_small(tot[2])
    return y[None], dx[None], gg, gb, gq, gqb, go, gob, gu, gub, gd, gdb

def solution(mesh):
    f = P("fsdp", "seq", None, None)
    ins = (f, P(None, None, "fsdp"), P(None, None, "fsdp"), P(None, None, "fsdp", None), P(None, None, None, "fsdp"), P(None, None, "fsdp", None),
        P(None, None, "fsdp"), P(None, "fsdp", None), P(None, "fsdp"), P(None, "fsdp", None), P(None, "fsdp"), f)
    return jax.shard_map(local, mesh=mesh, in_specs=ins, out_specs=(f, f) + ins[1:11], check_vma=False)
```

```python
import functools
import jax
import jax.numpy as jnp
from jax import lax
from jax.experimental import pallas as pl
from jax.experimental.pallas import tpu as pltpu
from jax.sharding import PartitionSpec as P
MESH = pl.DeviceIdType.MESH
bf16, f32 = jnp.bfloat16, jnp.float32
T, D, F = 256, 768, 3072
NN = (((1,), (0,)), ((), ()))
NT = (((1,), (1,)), ((), ()))
ORDERS = (("x", "y", "z"), ("y", "z", "x"), ("z", "x", "y"))
STORED = ("x", "z", "y")

def coords():
    f, s = lax.axis_index("fsdp"), lax.axis_index("seq")
    return {"x": f // 8, "y": f % 4, "z": ((f // 4) % 2) * 2 + s // 2}, s % 2

def dev(at, c):
    return (at["x"] * 8 + (at["z"] // 2) * 4 + at["y"], (at["z"] % 2) * 2 + c)

def moved(at, axis, by):
    return {**at, axis: (at[axis] + by + 4) % 4}

def greet(at, c):
    bar = pltpu.get_barrier_semaphore()
    other = moved(at, "z", 1 - 2 * (at["z"] % 2))
    peers = [dev(moved(at, a, d), c) for a in "xyz" for d in (1, -1)] + [dev(at, 1 - c), dev(other, 1 - c)]
    for p in peers:
        pl.semaphore_signal(bar, inc=1, device_id=p, device_id_type=MESH)
    pl.semaphore_wait(bar, len(peers))

def remote(src, dst, ssem, rsem, to):
    return pltpu.make_async_remote_copy(src, dst, ssem, rsem, device_id=to, device_id_type=MESH)

def index(sel):
    return tuple(pl.ds(0, 4) if v is None else pl.ds(*v) if isinstance(v, tuple) else v for v in sel)

class Gather:
    ROUNDS = 8
    def __init__(self, s, g, b, p, at, c, sems):
        self.s, self.g, self.b, self.p, self.at, self.c = s, g, b, p, at, c
        self.ssem, self.rsem, self.lsem = sems
        self.order, self.pending = ORDERS[p], []
    def ref(self, st, coord, half=None, c=None):
        sel = {}
        for i, a in enumerate(self.order):
            sel[a] = None if i < st else coord if i == st else self.at[a]
        if half is not None and st > 0:
            sel[[a for a in STORED if a in self.order[:st]][0]] = (2 * half, 2)
        ref = self.g.at[(self.b, self.c if c is None else c, self.p) + index(sel[a] for a in STORED)]
        return ref if half is None or st > 0 else ref.at[pl.ds(32 * half, 32 - 16 * half), :]
    def copy(self, src, dst, k, to):
        return remote(src, dst, self.ssem.at[self.b, self.p, k], self.rsem.at[self.b, self.p, k], to)
    def go(self, ref, k, to, src=None):
        cp = self.copy(ref if src is None else src, ref, k, to)
        cp.start()
        self.pending.append(cp)
    def got(self, ref, k):
        self.copy(ref, ref, k, dev(self.at, 1 - self.c)).wait_recv()
    def round(self, r):
        sib = dev(self.at, 1 - self.c)
        last = self.at[self.order[2]]
        if 0 < r < 7:
            st, ph = divmod(r - 1, 2)
            here = self.at[self.order[st]]
            if ph == 0:
                self.got(self.ref(st, (here + 3) % 4), 4 * st)
                self.got(self.ref(st, (here + 1) % 4), 4 * st + 1)
            else:
                for h in (0, 1):
                    self.got(self.ref(st, (here + 2) % 4, h), 4 * st + 2 + h)
        if r < 6:
            st, ph = divmod(r, 2)
            a = self.order[st]
            here = self.at[a]
            up, down = (dev(moved(self.at, a, d), self.c) for d in (1, -1))
            own = self.ref(st, here)
            if ph == 0:
                src = None
                if r == 0:
                    src = self.s.at[self.b, self.c, self.p, self.at["z"] % 2]
                    self.local = pltpu.make_async_copy(src, own, self.lsem.at[self.b, self.p])
                    self.local.start()
                if r == 2:
                    self.local.wait()
                self.go(own, 4 * st, up, src)
                self.go(own, 4 * st + 1, down, src)
                if st == 2:
                    self.go(own, 12, sib)
            else:
                self.go(self.ref(st, (here + 3) % 4, 0), 4 * st + 2, up)
                self.go(self.ref(st, (here + 1) % 4, 1), 4 * st + 3, down)
                if st == 2:
                    self.go(self.ref(2, (here + 3) % 4), 13, sib)
                    self.go(self.ref(2, (here + 1) % 4), 14, sib)
        if r == 6:
            self.go(self.ref(2, (last + 2) % 4), 15, sib)
        if r == 7:
            for k, by in ((12, 0), (13, 3), (14, 1), (15, 2)):
                self.got(self.ref(2, (last + by) % 4, c=1 - self.c), k)
    def end(self):
        for cp in self.pending:
            cp.wait_send()

class Point:
    def __init__(self, at, c, ssem, rsem):
        self.at, self.c, self.ssem, self.rsem, self.sends = at, c, ssem, rsem, []
    def send(self, src, dst, k, to):
        cp = remote(src, dst, self.ssem.at[k], self.rsem.at[k], to)
        cp.start()
        self.sends.append(cp)
    def got(self, ref, k):
        remote(ref, ref, self.ssem.at[k], self.rsem.at[k], dev(self.at, 1 - self.c)).wait_recv()
    def near(self, a, d):
        return dev(moved(self.at, a, d), self.c)
    def end(self):
        for cp in self.sends:
            cp.wait_send()

class SmallGather(Point):
    def __init__(self, s, gs, at, c, ssem, rsem, lsem):
        super().__init__(at, c, ssem, rsem)
        self.s, self.gs, self.lsem = s, gs, lsem
    def round(self, r):
        at, gs = self.at, self.gs
        x, y, zh = at["x"], at["y"], at["z"] // 2
        blk = lambda by: gs.at[(x + by + 4) % 4, zh, y]
        row = lambda by: gs.at[:, zh, (y + by + 4) % 4]
        if r == 0:
            self.local = pltpu.make_async_copy(self.s, blk(0), self.lsem)
            self.local.start()
            self.send(self.s, blk(0), 0, self.near("x", 1))
            self.send(self.s, blk(0), 1, self.near("x", -1))
        if r == 1:
            self.got(blk(-1), 0)
            self.send(blk(-1), blk(-1), 2, self.near("x", 1))
        if r == 2:
            self.got(blk(1), 1)
            self.got(blk(2), 2)
            self.local.wait()
            self.send(row(0), row(0), 3, self.near("y", 1))
            self.send(row(0), row(0), 4, self.near("y", -1))
        if r == 3:
            self.got(row(-1), 3)
            self.send(row(-1), row(-1), 5, self.near("y", 1))
        if r == 4:
            self.got(row(1), 4)
            self.got(row(2), 5)
            self.send(gs.at[:, zh], gs.at[:, zh], 6, dev({**at, "z": 3 - at["z"]}, self.c))
        if r == 5:
            self.got(gs.at[:, 1 - zh], 6)

class Reduce:
    def __init__(self, n, b, at, c, made, red, held, land, sums, sems):
        self.n, self.b, self.at, self.c = n, b, at, c
        self.made, self.red, self.held, self.land = made.at[n % made.shape[0]], red, held.at[n % held.shape[0]], land
        self.sums = [self.made.at[c]] + [q.at[n % q.shape[0]] for q in sums]
        self.ssem, self.rsem, self.lsem = sems
        self.sib = dev(at, 1 - c)
        self.pending = {}
    def block(self, p, st, by, half=None, base=None):
        order = ORDERS[p][::-1]
        sel = {a: None for a in STORED if a not in order[:st]}
        sel[order[st]] = (self.at[order[st]] + by + 4) % 4
        if half is not None and st < 2:
            sel[[a for a in sel if a != order[st]][0]] = (2 * half, 2)
        ref = (self.sums[st] if base is None else base).at[(p,) + index(sel.values())]
        return ref.at[pl.ds(32 * half, 32 - 16 * half), :] if half is not None and st == 2 else ref
    def arrival(self, p, st, k, half=None):
        if half is None:
            ref = self.land[st][0]
            return ref.at[self.n % ref.shape[0], p, k]
        ref = self.land[st][1]
        ref = ref.at[self.n % ref.shape[0], p]
        return ref.at[pl.ds(2 * half, 2)] if st < 2 else ref.at[pl.ds(32 * half, 32 - 16 * half), :]
    def copy(self, src, dst, p, k, to):
        return remote(src, dst, self.ssem.at[self.b, p, k], self.rsem.at[self.b, p, k], to)
    def send(self, group, *a):
        cp = self.copy(*a)
        cp.start()
        self.pending.setdefault(group, []).append(cp)
    def got(self, ref, p, k):
        self.copy(ref, ref, p, k, self.sib).wait_recv()
    def sent(self, group):
        for cp in self.pending.pop(group, []):
            cp.wait_send()
    def near(self, p, st, by):
        return dev(moved(self.at, ORDERS[p][2 - st], by), self.c)
    def halves(self, st, p):
        self.send(st, self.block(p, st, 2, 0), self.arrival(p, st, 2, 0), p, 4 * st + 0, self.near(p, st, 1))
        self.send(st, self.block(p, st, 2, 1), self.arrival(p, st, 2, 1), p, 4 * st + 1, self.near(p, st, -1))
    def give(self):
        for i, by in enumerate((2, 1, -1, 0)):
            for p in range(3):
                src = self.block(p, 0, by, base=self.made.at[1 - self.c])
                self.send(0, src, self.block(p, 0, by, base=self.held), p, 12 + i, self.sib)
    def add_held(self, p, by, i):
        mine, held = self.block(p, 0, by), self.block(p, 0, by, base=self.held)
        self.got(held, p, 12 + i)
        mine[...] = mine[...] + held[...]
    def take(self):
        for p in range(3):
            self.add_held(p, 2, 0)
            self.halves(0, p)
        for i, by in ((1, 1), (2, -1), (3, 0)):
            for p in range(3):
                self.add_held(p, by, i)
    def add_halves(self, st):
        for p in range(3):
            for half, by in ((0, 1), (1, -1)):
                dst, src = self.block(p, st, by, half), self.arrival(p, st, 2, half)
                self.got(src, p, 4 * st + half)
                dst[...] = dst[...] + src[...]
    def wholes(self, st):
        for p in range(3):
            self.send(st, self.block(p, st, 1), self.arrival(p, st, 0), p, 4 * st + 2, self.near(p, st, 1))
            self.send(st, self.block(p, st, -1), self.arrival(p, st, 1), p, 4 * st + 3, self.near(p, st, -1))
    def add_wholes(self, st):
        for p in range(3):
            s0, s1 = self.arrival(p, st, 0), self.arrival(p, st, 1)
            self.got(s0, p, 4 * st + 2)
            self.got(s1, p, 4 * st + 3)
            total = self.block(p, st, 0)[...].astype(f32) + s0[...].astype(f32) + s1[...].astype(f32)
            self.sums[st + 1][p] = total.astype(bf16)
            if st < 2:
                self.halves(st + 1, p)
    def peers(self):
        other = moved(self.at, "z", 1 - 2 * (self.at["z"] % 2))
        zl = self.at["z"] % 2
        return ((dev(other, self.c), self.c, 1 - zl), (dev(other, 1 - self.c), 1 - self.c, 1 - zl), (self.sib, 1 - self.c, zl))
    def share(self):
        own, mine = self.sums[3], self.red.at[self.b, self.c, :, self.at["z"] % 2]
        self.local = pltpu.make_async_copy(own, mine, self.lsem.at[self.b])
        self.local.start()
        for i, (to, _, _) in enumerate(self.peers()):
            self.send(3, own, mine, i, 16, to)
    def collect(self):
        self.local.wait()
        for i, (_, c, zl) in enumerate(self.peers()):
            self.got(self.red.at[self.b, c, :, zl], i, 16)
    def end(self):
        for g in list(self.pending):
            self.sent(g)

class SmallReduce(Point):
    def __init__(self, sg, tot, bx, by, bz, at, c, ssem, rsem):
        super().__init__(at, c, ssem, rsem)
        self.sg, self.tot, self.bx, self.by, self.bz = sg, tot, bx, by, bz
    def round(self, r):
        at, sg, tot, bx, by, bz = self.at, self.sg, self.tot, self.bx, self.by, self.bz
        x, y, z = at["x"], at["y"], at["z"]
        zh, zl = z // 2, z % 2
        blk = lambda d: sg.at[(x + d + 4) % 4]
        row = lambda d: sg.at[x, :, (y + d + 4) % 4]
        def add(dst, *more):
            v = dst[...].astype(f32)
            for q in more:
                v = v + q[...].astype(f32)
            dst[...] = v.astype(bf16)
        if r == 0:
            self.send(blk(2), bx.at[0], 0, self.near("x", 1))
            self.send(blk(-1), bx.at[1], 1, self.near("x", -1))
        if r == 1:
            self.got(bx.at[0], 0)
            add(blk(1), bx.at[0])
            self.send(blk(1), bx.at[2], 2, self.near("x", 1))
        if r == 2:
            self.got(bx.at[1], 1)
            self.got(bx.at[2], 2)
            add(blk(0), bx.at[1], bx.at[2])
            self.send(row(2), by.at[0], 3, self.near("y", 1))
            self.send(row(-1), by.at[1], 4, self.near("y", -1))
        if r == 3:
            self.got(by.at[0], 3)
            add(row(1), by.at[0])
            self.send(row(1), by.at[2], 5, self.near("y", 1))
        if r == 4:
            self.got(by.at[1], 4)
            self.got(by.at[2], 5)
            add(row(0), by.at[1], by.at[2])
            self.send(sg.at[x, 1 - zh, y], bz.at[0], 6, dev({**at, "z": 3 - z}, self.c))
        if r == 5:
            self.got(bz.at[0], 6)
            tot[0] = (sg[x, zh, y].astype(f32) + bz[0].astype(f32)).astype(bf16)
            self.send(tot.at[0], bz.at[1], 7, self.near("z", 1 - 2 * zl))
        if r == 6:
            self.got(bz.at[1], 7)
            tot[1] = (tot[0].astype(f32) + bz[1].astype(f32)).astype(bf16)
            self.send(tot.at[1], bz.at[2], 8, dev(at, 1 - self.c))
        if r == 7:
            self.got(bz.at[2], 8)
            tot[2] = (tot[1].astype(f32) + bz[2].astype(f32)).astype(bf16)

def exchange(n, src, dst, to_places, sems):
    f, s = lax.axis_index("fsdp"), lax.axis_index("seq")
    ssem, rsem, lsem = sems
    cps = []
    for i in (2, 3, 1, 0):
        t = (s + i) % 4
        if to_places:
            a, b = src.at[:, pl.ds(pl.multiple_of(t * 16, 16), 16), :], dst.at[pl.ds(4 * s, 4)]
        else:
            a, b = src.at[pl.ds(4 * t, 4)], dst.at[:, pl.ds(pl.multiple_of(s * 16, 16), 16), :]
        cp = pltpu.make_async_copy(a, b, lsem.at[n]) if i == 0 else remote(a, b, ssem.at[n, i - 1], rsem.at[n, i - 1], (f, t))
        cp.start()
        cps.append(cp)
    return cps

def finish(cps):
    for cp in cps:
        cp.wait()

def dot(a, b, dims=NN):
    return lax.dot_general(a, b, dims, preferred_element_type=f32)

def iota(shape, dim):
    return lax.broadcasted_iota(jnp.int32, shape, dim)

def chunk_at(m):
    return m // 6, (m // 2) % 3, m % 2

def cols(n, w=256):
    return slice(w * n, w * n + w)

def stats(x):
    xc = x - jnp.mean(x, axis=-1, keepdims=True)
    r = lax.rsqrt(jnp.mean(xc * xc, axis=-1, keepdims=True) + 1e-6)
    return xc * r, r

def norm_rows(u, gain, bias, a):
    for i in range(8):
        at = cols(i, 32)
        n, _ = stats(u[at, :].astype(f32))
        a[at, :] = (n * gain + bias).astype(bf16)

def norm_back(u, gain, da, du):
    sg = sb = jnp.zeros((8, D), f32)
    for i in range(8):
        at = cols(i, 32)
        n, r = stats(u[at, :].astype(f32))
        d = da[at, :]
        sg = sg + jnp.sum((d * n).reshape(4, 8, D), axis=0)
        sb = sb + jnp.sum(d.reshape(4, 8, D), axis=0)
        dn = d * gain
        c1 = jnp.mean(dn, axis=-1, keepdims=True)
        c2 = jnp.mean(dn * n, axis=-1, keepdims=True)
        du[at, :] = du[at, :] + r * (dn - c1 - n * c2)
    return jnp.sum(sg, axis=0, keepdims=True), jnp.sum(sb, axis=0, keepdims=True)

def column_sum(x):
    return dot(jnp.ones((8, T), bf16), x)[0:1]

def lanes(h, value):
    return jnp.where(iota((1, 128), 1) // 64 == h, value, 0.0).astype(bf16)

def attend(qkv, mask, o, lse_t, acc):
    lane = iota((1, 128), 1)
    for hp in range(6):
        q, k, v = (qkv[:, cols(6 * i + hp, 128)] for i in range(3))
        mixed = None
        for h in range(2):
            s = dot(q, k * lanes(h, 0.125), NT) + mask[...].astype(f32)
            top = jnp.max(s, axis=-1, keepdims=True)
            e = jnp.exp(s - top)
            tot = jnp.sum(e, axis=-1, keepdims=True)
            part = dot((e * (1.0 / tot)).astype(bf16), v * lanes(h, 1.0))
            mixed = part if mixed is None else mixed + part
            lse = top + jnp.log(tot)
            acc[...] = jnp.where(lane == 2 * hp + h, lse, 0.0 if hp + h == 0 else acc[...])
        o[:, cols(hp, 128)] = mixed.astype(bf16)
    lse_t[...] = acc[...].T[0:16, :]

def attend_back(qkv, mask, lse_t, do, delta_t, g, kt, dqt):
    kt[...] = (qkv[:, D:2 * D].astype(f32) * 0.125).T.astype(bf16)
    for hp in range(6):
        q, k, v = (qkv[:, cols(6 * i + hp, 128)] for i in range(3))
        d = do[:, cols(hp, 128)]
        dk = dv = None
        for h in range(2):
            row = slice(2 * hp + h, 2 * hp + h + 1)
            pt = jnp.exp(dot(k * lanes(h, 0.125), q, NT) + mask[...].astype(f32) - lse_t[row, :])
            dpt = dot(v * lanes(h, 1.0), d, NT)
            dst = (pt * (dpt - delta_t[row, :])).astype(bf16)
            a = dot(pt.astype(bf16), d * lanes(h, 1.0))
            b = dot(dst, q * lanes(h, 0.125))
            dv = a if dv is None else dv + a
            dk = b if dk is None else dk + b
            rows = cols(2 * hp + h, 64)
            dqt[rows, :] = dot(kt[rows, :], dst).astype(bf16)
        g[:, cols(6 + hp, 128)] = dk.astype(bf16)
        g[:, cols(12 + hp, 128)] = dv.astype(bf16)
    g[:, 0:D] = dqt[...].T

def head_sums(do, o, out):
    one = jnp.where(iota((16, D), 1) // 64 == iota((16, D), 0), 1.0, 0.0).astype(bf16)
    x = do[...].astype(f32) * o[...].astype(f32)
    hi = x.astype(bf16)
    lo = (x - hi.astype(f32)).astype(bf16)
    out[...] = dot(one, hi, NT) + dot(one, lo, NT)

def set_masks(masks):
    r0, r1 = iota((T, T), 0), iota((T, T), 1)
    masks[0] = jnp.where(r0 // 64 == r1 // 64, 0.0, -1e30).astype(bf16)
    masks[1] = jnp.where(r0 % 16 == r1 % 16, 0.0, -1e30).astype(bf16)

def spread(gs, vec, upb):
    place = jnp.where((iota((128, D), 1) % 24 == iota((128, D), 0)), 1.0, 0.0).astype(bf16)
    own = iota((32, 1, D), 2) // 24 == iota((32, 1, D), 0)
    place4 = jnp.where((iota((128, F), 1) % 96 == iota((128, F), 0)), 1.0, 0.0).astype(bf16)
    own4 = iota((32, F), 1) // 96 == iota((32, F), 0)
    for l in range(2):
        x = gs[:, :, :, pl.ds(16 * l, 16), :].reshape(32, 16, 128)
        y = dot(x.reshape(512, 128), place).reshape(32, 16, D)
        vec[l] = jnp.sum(jnp.where(own, y, 0.0), axis=0)
        z = dot(x.astype(f32)[:, 13, :].astype(bf16), place4)
        upb[l] = jnp.sum(jnp.where(own4, z, 0.0), axis=0, keepdims=True)

def collect(l, vecg, upg, sg):
    place = jnp.where((iota((D, 128), 0) % 24 == iota((D, 128), 1)), 1.0, 0.0).astype(bf16)
    own = iota((32, 1, D), 2) // 24 == iota((32, 1, D), 0)
    x = jnp.where(own, vecg[l][None], 0.0).astype(bf16).reshape(512, D)
    y = dot(x, place).reshape(32, 16, 128)
    place4 = jnp.where((iota((F, 128), 0) % 96 == iota((F, 128), 1)), 1.0, 0.0).astype(bf16)
    own4 = iota((32, F), 1) // 96 == iota((32, F), 0)
    z = dot(jnp.where(own4, upg[l], 0.0).astype(bf16), place4)
    y = jnp.where(iota((32, 16, 128), 1) == 13, z[:, None, :], y)
    sg[:, :, :, pl.ds(16 * l, 16), :] = y.astype(bf16).reshape(4, 2, 4, 16, 128)

def unpack_chunk(st, w, lo, hi):
    for i in range(16):
        x = st[pl.ds(2 * i, 2)].astype(f32).reshape(2, 2, 24, 128)
        at = cols(i, 48)
        w[at, pl.ds(lo, 128)] = x[:, 0].reshape(48, 128).astype(bf16)
        w[at, pl.ds(hi, 128)] = x[:, 1].reshape(48, 128).astype(bf16)

def pack_pair(r):
    a, b = r[:, :128].reshape(32, 24, 128), r[:, 128:].reshape(32, 24, 128)
    return jnp.concatenate([a, b], axis=1).astype(bf16).reshape(4, 2, 4, 48, 128)

def pair(x, lo, hi):
    return jnp.concatenate([x[:, lo:lo + 128], x[:, hi:hi + 128]], axis=1)

def pack_shard(b, qkv, out, up, down, s):
    l, j = divmod(b, 4)
    for m in range(12):
        if j == 3:
            x = down[l, cols(m % 2, 48), cols(m // 2, 128)]
        else:
            w, n, half = (up.at[l], m, 1536) if j == 2 else (qkv.at[l, j], m, 1152) if m < 9 else (out.at[l, j], m - 9, 384)
            lo, hi = w[:, cols(n, 128)], w[:, half + 128 * n:half + 128 * n + 128]
            x = jnp.concatenate([lo.astype(f32), hi.astype(f32)], axis=0).astype(bf16)
        s[(b,) + chunk_at(m)] = x

def unpack_shard(b, s, qkv, out, up, down):
    l, j = divmod(b, 4)
    for m in range(12):
        y = s[(b,) + chunk_at(m)].astype(f32)
        if j == 3:
            down[l, cols(m % 2, 48), cols(m // 2, 128)] = y
        else:
            w, n, half = (up.at[l], m, 1536) if j == 2 else (qkv.at[l, j], m, 1152) if m < 9 else (out.at[l, j], m - 9, 384)
            w[:, cols(n, 128)] = y[:24]
            w[:, half + 128 * n:half + 128 * n + 128] = y[24:]

def pack_vectors(gain, bias, qb, ob, ub, db, wide, s):
    wide[...] = jnp.zeros_like(wide)
    for l in range(2):
        r = 16 * l
        wide[r:r + 3, 0:24] = gain[l].astype(f32)
        wide[r + 3:r + 6, 0:24] = bias[l].astype(f32)
        for i in range(4):
            wide[r + 6 + i:r + 7 + i, 0:24] = qb[l, i // 2, i % 2:i % 2 + 1].astype(f32)
        wide[r + 10:r + 12, 0:24] = ob[l].astype(f32)
        wide[r + 12:r + 13, 0:24] = db[l:l + 1].astype(f32)
        wide[r + 13:r + 14, 0:96] = ub[l:l + 1].astype(f32)
    s[...] = wide[...].astype(bf16)

def unpack_vectors(wide, gain, bias, qb, ob, ub, db):
    for l in range(2):
        r = 16 * l
        gain[l] = wide[r:r + 3, 0:24]
        bias[l] = wide[r + 3:r + 6, 0:24]
        for i in range(4):
            qb[l, i // 2, i % 2:i % 2 + 1] = wide[r + 6 + i:r + 7 + i, 0:24]
        ob[l] = wide[r + 10:r + 12, 0:24]
        db[l:l + 1] = wide[r + 12:r + 13, 0:24]
        ub[l:l + 1] = wide[r + 13:r + 14, 0:96]


OFFS = (0, 2, 3, 4, 5, 6, 7, 8)

def forward_kernel(clips, gain_i, bias_i, qkv_i, qb_i, out_i, ob_i, up_i, ub_i, down_i, db_i, cot, gw, wqkv_o, wo_o, wup_o, qkv_o, o_o, lse_o, u_o, u2_o, h_o, gp_o, vec_o, cot_o,
                   s, ss, wide, gs, wqkv, wo, wup, wdn, stage, su, sqkv, so, slse, su2, sh, sgp, vec, upb, masks, a_buf, acc, x3f, x3p, rp, rf,
                   gss, grs, gls, sss, srs, sls, ess, ers, els, wsem, osem):
    at, c = coords()
    greet(at, c)
    small = SmallGather(ss, gs, at, c, sss, srs, sls.at[0])
    parts = [[Gather(s, gw, b, p, at, c, (gss, grs, gls)) for p in range(3)] for b in range(8)]
    state = {"t": 0, "out": 0}
    ready, fetched, unpacked, done = set(), {}, set(), set()
    esems = (ess, ers, els)
    saves = {}

    def save(key, src, dst):
        cp = pltpu.make_async_copy(src, dst, osem.at[state["out"]])
        state["out"] += 1
        cp.start()
        saves[key] = cp

    def fetch(b):
        l, j = divmod(b, 4)
        gz = gw.reshape(8, 2, 3, 4, 2, 2, 4, 48, 128)
        cps = []
        for m in range(12):
            ci, p, zl = chunk_at(m)
            dst = stage.at[b % 2, m] if j < 3 else wdn.at[:, :, :, m % 2, :, pl.ds(128 * (m // 2), 128)]
            cp = pltpu.make_async_copy(gz.at[b, ci, p, :, :, zl], dst, wsem.at[b % 2, m])
            cp.start()
            cps.append(cp)
        fetched[b] = cps

    def try_fetch():
        for b in range(8):
            if b < 7 and b in ready and b not in fetched and (b < 2 or b - 2 in unpacked) and (b % 4 < 3 or b < 4 or b - 4 in done):
                fetch(b)

    def slot():
        t = state["t"]
        if t > OFFS[-1] + 7:
            return
        if t == 0:
            pack_vectors(gain_i, bias_i, qb_i, ob_i, ub_i, db_i, wide, ss)
        if t < 6:
            small.round(t)
        for b in range(8):
            if t == OFFS[b]:
                pack_shard(b, qkv_i, out_i, up_i, down_i, s)
        for b in reversed(range(8)):
            r = t - OFFS[b]
            if 0 <= r < 8:
                for p in range(3):
                    parts[b][p].round(r)
                if r == 7:
                    ready.add(b)
        state["t"] += 1
        try_fetch()

    def poll(b):
        if b < 7 and state["t"] <= OFFS[b + 1] + 7:
            slot()

    def weights(b):
        if b in unpacked:
            return
        l, j = divmod(b, 4)
        while b not in ready:
            slot()
        try_fetch()
        cps = fetched[b]
        if j < 3 and l:
            saves.pop((0, j)).wait()
            if j < 2:
                saves.pop((0, j, 0)).wait()
        for m in range(12):
            cps[m].wait()
            if j == 3:
                continue
            st = stage.at[b % 2, m].reshape(32, 48, 128)
            if j == 2:
                unpack_chunk(st, wup, 128 * m, 1536 + 128 * m)
            elif m < 9:
                unpack_chunk(st, wqkv.at[j], 128 * m, 1152 + 128 * m)
            else:
                unpack_chunk(st, wo.at[j], 128 * (m - 9), 384 + 128 * (m - 9))
        unpacked.add(b)
        if j < 2:
            save((l, j), wqkv.at[j], wqkv_o.at[l, j])
            save((l, j, 0), wo.at[j], wo_o.at[l, j])
        elif j == 2:
            save((l, j), wup, wup_o.at[l])
        try_fetch()

    def branch(l, k, put):
        b = 4 * l + k
        weights(b)
        u, v = su.at[l, k], vec.at[l]
        norm_rows(u, v[k:k + 1], v[3 + k:4 + k], a_buf)
        save(("u", l, k), u, u_o.at[l, k])
        for n in range(9):
            y = dot(a_buf[...], wqkv[k, :, cols(n)])
            if n // 3 != 1:
                y = y + v[6 + 2 * k + n // 6:7 + 2 * k + n // 6, cols(n % 3)]
            sqkv[l, k, :, cols(n)] = y.astype(bf16)
        save(("q", l, k), sqkv.at[l, k], qkv_o.at[l, k])
        poll(b)
        attend(sqkv.at[l, k], masks.at[k], so.at[l, k], slse.at[l, k], acc)
        save(("o", l, k), so.at[l, k], o_o.at[l, k])
        for n in range(3):
            put(n, u[:, cols(n)].astype(f32) + dot(so[l, k], wo[k, :, cols(n)]) + v[10 + k:11 + k, cols(n)])
        done.add(b)

    def layer(l):
        def put1(n, y):
            x3f[l, :, :, cols(n)] = y.astype(bf16).reshape(4, 64, 256)
        branch(l, 0, put1)
        cps = exchange(1 + 2 * l, x3f.at[l], rp.at[1 + l], True, esems)
        weights(4 * l + 1)
        finish(cps)
        su[l, 1] = rp[1 + l].reshape(T, D)
        def put2(n, y):
            su2[l, :, cols(n)] = y
        branch(l, 1, put2)
        save(("u2", l), su2.at[l], u2_o.at[l])
        poll(4 * l + 1)
        weights(4 * l + 2)
        v = vec.at[l]
        norm_rows(su2.at[l], v[2:3], v[5:6], a_buf)
        for n in range(12):
            z = dot(a_buf[...], wup[:, cols(n)]) + upb[l, :, cols(n)]
            cdf = 0.5 * (1.0 + lax.erf(z * 0.7071067811865476))
            sh[l, :, cols(n)] = (z * cdf).astype(bf16)
            sgp[l, :, cols(n)] = (cdf + z * (0.3989422804014327 * jnp.exp(-0.5 * z * z))).astype(bf16)
            if n == 5:
                poll(4 * l + 2)
        save(("h", l), sh.at[l], h_o.at[l])
        save(("gp", l), sgp.at[l], gp_o.at[l])
        done.add(4 * l + 2)
        if l == 1:
            return
        poll(2)
        weights(3)
        for n in range(3):
            y = su2[l, :, cols(n)] + dot(sh[l], wdn[:, :, :, :, :, cols(n)].reshape(F, 256)) + v[12:13, cols(n)]
            x3p[:, :, cols(n)] = y.astype(bf16).reshape(16, 16, 256)
        done.add(3)
        cps = exchange(2, x3p, rf, False, esems)
        weights(4)
        finish(cps)
        su[1, 0] = rf[...].reshape(T, D)

    slot()
    first = exchange(0, cot, rp.at[0], True, esems)
    set_masks(masks)
    su[0, 0] = clips[...].reshape(T, D)
    for _ in range(5):
        slot()
    spread(gs, vec, upb)
    save("vec", vec, vec_o)
    layer(0)
    finish(first)
    save("cot", rp.at[0], cot_o)
    layer(1)
    save("lse", slse, lse_o)
    while 7 not in ready:
        slot()
    for ps in parts:
        for g in ps:
            g.end()
    small.end()
    for cp in saves.values():
        cp.wait()

def forward(*args, cid=0):
    V = pltpu.VMEM
    S = lambda *shape: pltpu.SemaphoreType.DMA(shape)
    vm, hbm = pl.BlockSpec(memory_space=pltpu.VMEM), pl.BlockSpec(memory_space=pl.ANY)
    o = lambda *shape, dt=bf16: jax.ShapeDtypeStruct(shape, dt)
    outs = (o(8, 2, 3, 4, 4, 4, 48, 128), o(2, 2, D, 3 * D), o(2, 2, D, D), o(2, D, F),
            o(2, 2, T, 3 * D), o(2, 2, T, D), o(2, 2, 16, T, dt=f32), o(2, 2, T, D), o(2, T, D, dt=f32), o(2, T, F), o(2, T, F),
            o(2, 16, D, dt=f32), o(16, 16, D))
    scratch = [
        V((8, 2, 3, 2, 48, 128), bf16), V((32, 128), bf16), V((32, 128), f32), V((4, 2, 4, 32, 128), bf16), V((2, D, 3 * D), bf16), V((2, D, D), bf16), V((D, F), bf16), V((4, 2, 4, 2, 48, D), bf16),
        V((2, 12, 4, 2, 4, 48, 128), bf16), V((2, 2, T, D), bf16), V((2, 2, T, 3 * D), bf16), V((2, 2, T, D), bf16), V((2, 2, 16, T), f32),
        V((2, T, D), f32), V((2, T, F), bf16), V((2, T, F), bf16), V((2, 16, D), f32), V((2, 1, F), f32), V((2, T, T), bf16),
        V((T, D), bf16), V((T, 128), f32), V((2, 4, 64, D), bf16), V((16, 16, D), bf16), V((3, 16, 16, D), bf16), V((4, 64, D), bf16),
        S(8, 3, 16), S(8, 3, 16), S(8, 3), S(7), S(7), S(1), S(4, 3), S(4, 3), S(4), S(2, 12), S(40)]
    return pl.pallas_call(forward_kernel, out_shape=outs, in_specs=[vm] * 12, out_specs=tuple([hbm] * 13), scratch_shapes=scratch,
        compiler_params=pltpu.CompilerParams(collective_id=cid, has_side_effects=True, vmem_limit_bytes=63 << 20), name="forward")(*args)


def backward_kernel(gw, wqkv_i, wo_i, wup_i, qkv_i, o_i, lse_i, u_i, u2_i, h_i, gp_i, vec, cot_i, out, dclips, red, total,
                    wqkv, wo, wup, wdn, sqkv, so, slse, su, su2, sh, sgp, masks, a_buf, t_buf, e_buf, g_buf, da, du, dqt, delta,
                    vecg, upg, made_g, tot, x3p, x3f, rf, rp, held, f0, h0, f1, h1, f2, h2, s1, s2, s3, sg, bx, by, bz,
                    rss, rrs, rls, sss, srs, ess, ers, els, isem, osem):
    at, c = coords()
    greet(at, c)
    esems = (ess, ers, els)
    slots = made_g.shape[0]
    grads = made_g.reshape(slots, 2, 3, 4, 2, 2, 4, 48, 128)
    subs = [Reduce(n, 7 - n, at, c, made_g, red, held, ((f0, h0), (f1, h1), (f2, h2)), (s1, s2, s3), (rss, rrs, rls)) for n in range(8)]
    small = SmallReduce(sg, tot, bx, by, bz, at, c, sss, srs)
    state = {"t": 0, "in": 0}
    loads = {}

    def slot():
        t = state["t"]
        state["t"] += 1
        step = {t - n: subs[n] for n in range(8) if 1 <= t - n <= 8}
        if 2 in step:
            step[2].add_halves(0)
        if 1 in step:
            step[1].take()
        if 2 in step:
            step[2].wholes(0)
        if 8 in step:
            step[8].collect()
        for st in (2, 1, 0):
            if 2 * st + 4 in step and st < 2:
                step[2 * st + 4].add_halves(st + 1)
                step[2 * st + 4].wholes(st + 1)
            if 2 * st + 3 in step:
                q = step[2 * st + 3]
                if q.n >= 2:
                    subs[q.n - 2].sent(st + 1)
                q.add_wholes(st)
                if st == 2:
                    q.share()

    def load(key, src, dst):
        cp = pltpu.make_async_copy(src, dst, isem.at[state["in"]])
        state["in"] += 1
        cp.start()
        loads.setdefault(key, []).append(cp)

    def have(key):
        for cp in loads.pop(key, []):
            cp.wait()

    def load_mlp(l):
        load((l, "h"), h_i.at[l], sh)
        gz = gw.reshape(8, 2, 3, 4, 2, 2, 4, 48, 128)
        for m in range(12):
            ci, p, zl = chunk_at(m)
            load((l, "dn"), gz.at[4 * l + 3, ci, p, :, :, zl], wdn.at[:, :, :, m % 2, :, pl.ds(128 * (m // 2), 128)])
        load((l, "gp"), gp_i.at[l], sgp)
        load((l, "up"), wup_i.at[l], wup)
        load((l, "u2"), u2_i.at[l], su2)

    def load_branch(l, k):
        load((l, k, "w"), wo_i.at[l, k], wo.at[k])
        load((l, k, "q"), qkv_i.at[l, k], sqkv.at[k])
        load((l, k, "q"), o_i.at[l, k], so.at[k])
        load((l, k, "w"), wqkv_i.at[l, k], wqkv.at[k])
        load((l, k, "q"), u_i.at[l, k], su.at[k])

    def claim(b):
        n = 7 - b
        while state["t"] <= n:
            slot()
        if n >= slots:
            subs[n - slots].sent(0)

    def put(b, m, value, x=None):
        ci, p, zl = chunk_at(m)
        if x is None:
            grads[(7 - b) % slots, ci, p, :, :, zl] = value
        else:
            grads[(7 - b) % slots, ci, p, x, :, zl] = value

    def made(b):
        subs[7 - b].give()

    def mlp(l):
        v = vec.at[l]
        e = e_buf.at[0]
        e[...] = du[...].astype(bf16)
        if l == 1:
            mlp_down_grads(l)
        have((l, "dn"))
        have((l, "gp"))
        for i in range(8):
            w = wdn[i // 2, i % 2].reshape(384, D)
            sgp[:, cols(i, 384)] = (dot(e[...], w, NT) * sgp[:, cols(i, 384)].astype(f32)).astype(bf16)
        have((l, "up"))
        for n in range(3):
            da[:, cols(n)] = dot(sgp[...], wup[cols(n), :], NT)
        have((l, "u2"))
        dg, db = norm_back(su2, v[2:3], da, du)
        vecg[l, 2:3, :] = dg
        vecg[l, 5:6, :] = db
        if l == 0:
            mlp_down_grads(l)

    def mlp_down_grads(l):
        e = e_buf.at[0]
        have((l, "h"))
        claim(4 * l + 3)
        for i in range(4):
            t_buf[...] = sh[:, cols(i, 768)].T
            for n in range(3):
                r = dot(t_buf[...], e[:, cols(n)]).astype(bf16).reshape(2, 4, 2, 48, 256)
                for q in range(4):
                    put(4 * l + 3, 4 * n + q, r[:, :, q % 2, :, cols(q // 2, 128)], i)
        vecg[l, 12:13, :] = column_sum(e[...])
        made(4 * l + 3)

    def mlp_up_grads(l):
        v = vec.at[l]
        norm_rows(su2, v[2:3], v[5:6], a_buf)
        t_buf[...] = a_buf[...].T
        claim(4 * l + 2)
        for m in range(12):
            put(4 * l + 2, m, pack_pair(dot(t_buf[...], pair(sgp, 128 * m, 1536 + 128 * m))))
        made(4 * l + 2)
        upg[l] = column_sum(sgp[...])

    def branch(l, k):
        v = vec.at[l]
        e = e_buf.at[k]
        e[...] = du[...].astype(bf16)
        have((l, k, "w"))
        have((l, k, "q"))
        for n in range(3):
            a_buf[:, cols(n)] = dot(e[...], wo[k, cols(n), :], NT).astype(bf16)
        head_sums(a_buf, so.at[k], delta)
        attend_back(sqkv.at[k], masks.at[k], slse.at[l, k], a_buf, delta, g_buf, t_buf, dqt)
        if l + k == 0:
            branch_grads(0, 0)
        for n in range(3):
            da[:, cols(n)] = dot(g_buf[...], wqkv[k, cols(n), :], NT)
        dg, db = norm_back(su.at[k], v[k:k + 1], da, du)
        vecg[l, k:k + 1, :] = dg
        vecg[l, 3 + k:4 + k, :] = db

    def branch_grads(l, k):
        v = vec.at[l]
        e = e_buf.at[k]
        claim(4 * l + k)
        t_buf[...] = so[k].T
        for i in range(3):
            put(4 * l + k, 9 + i, pack_pair(dot(t_buf[...], pair(e, 128 * i, 384 + 128 * i))))
        norm_rows(su.at[k], v[k:k + 1], v[3 + k:4 + k], a_buf)
        t_buf[...] = a_buf[...].T
        for m in range(9):
            put(4 * l + k, m, pack_pair(dot(t_buf[...], pair(g_buf, 128 * m, 1152 + 128 * m))))
        made(4 * l + k)
        vecg[l, 10 + k:11 + k, :] = column_sum(e[...])
        vecg[l, 6 + 2 * k:7 + 2 * k, :] = column_sum(g_buf[:, 0:D])
        vecg[l, 7 + 2 * k:8 + 2 * k, :] = column_sum(g_buf[:, 2 * D:3 * D])

    load(("du",), cot_i, rp)
    load_mlp(1)
    load(("lse",), lse_i, slse)
    load_branch(1, 1)
    load_branch(1, 0)
    set_masks(masks)
    vecg[...] = jnp.zeros_like(vecg)
    have(("du",))
    du[...] = rp[...].reshape(T, D).astype(f32)
    have(("lse",))
    for l in (1, 0):
        mlp(l)
        branch(l, 1)
        x3p[...] = du[...].astype(bf16).reshape(16, 16, D)
        cps = exchange(1 + l, x3p, rf, False, esems)
        mlp_up_grads(l)
        branch_grads(l, 1)
        if l == 1:
            load_branch(0, 1)
        finish(cps)
        du[...] = rf[...].reshape(T, D).astype(f32)
        branch(l, 0)
        if l == 1:
            x3f[...] = du[...].astype(bf16).reshape(4, 64, D)
            cps = exchange(3, x3f, rp, True, esems)
            for n in range(3):
                y = su2[:, cols(n)] + dot(sh[...], wdn[:, :, :, :, :, cols(n)].reshape(F, 256)) + vec[1, 12:13, cols(n)]
                x3p[:, :, cols(n)] = y.astype(bf16).reshape(16, 16, 256)
            last = exchange(0, x3p, out, False, esems)
            load_mlp(0)
            branch_grads(l, 0)
            load_branch(0, 0)
            finish(cps)
            finish(last)
            du[...] = rp[...].reshape(T, D).astype(f32)
        collect(l, vecg, upg, sg)
    x3f[...] = du[...].astype(bf16).reshape(4, 64, D)
    last = [pltpu.make_async_copy(x3f, dclips, osem.at[0])]
    last[0].start()
    for r in range(8):
        small.round(r)
        slot()
    total[...] = tot[2]
    finish(last)
    for s in subs:
        s.end()
    small.end()

def backward(*args, cid=1):
    V = pltpu.VMEM
    S = lambda *shape: pltpu.SemaphoreType.DMA(shape)
    vm, hbm = pl.BlockSpec(memory_space=pltpu.VMEM), pl.BlockSpec(memory_space=pl.ANY)
    sd = lambda *shape, dt=bf16: jax.ShapeDtypeStruct(shape, dt)
    outs = (sd(4, 64, D), sd(4, 64, D), sd(8, 2, 3, 2, 48, 128), sd(32, 128))
    scratch = [
        V((2, D, 3 * D), bf16), V((2, D, D), bf16), V((D, F), bf16), V((4, 2, 4, 2, 48, D), bf16),
        V((2, T, 3 * D), bf16), V((2, T, D), bf16), V((2, 2, 16, T), f32), V((2, T, D), bf16), V((T, D), f32), V((T, F), bf16), V((T, F), bf16),
        V((2, T, T), bf16), V((T, D), bf16), V((D, T), bf16), V((2, T, D), bf16), V((T, 3 * D), bf16), V((T, D), f32), V((T, D), f32), V((D, T), bf16), V((16, T), f32),
        V((2, 16, D), f32), V((2, 1, F), f32), V((3, 2, 3, 4, 4, 4, 48, 128), bf16), V((3, 32, 128), bf16),
        V((16, 16, D), bf16), V((4, 64, D), bf16), V((4, 64, D), bf16), V((16, 16, D), bf16),
        V((2, 3, 4, 4, 4, 48, 128), bf16), V((3, 3, 2, 4, 4, 48, 128), bf16), V((2, 3, 4, 4, 48, 128), bf16), V((2, 3, 2, 4, 48, 128), bf16), V((2, 3, 4, 48, 128), bf16), V((2, 3, 2, 48, 128), bf16), V((2, 3, 48, 128), bf16),
        V((2, 3, 4, 4, 48, 128), bf16), V((2, 3, 4, 48, 128), bf16), V((2, 3, 48, 128), bf16),
        V((4, 2, 4, 32, 128), bf16), V((3, 2, 4, 32, 128), bf16), V((3, 2, 32, 128), bf16), V((3, 32, 128), bf16),
        S(8, 3, 17), S(8, 3, 17), S(8), S(9), S(9), S(4, 3), S(4, 3), S(4), S(64), S(1)]
    return pl.pallas_call(backward_kernel, out_shape=outs, in_specs=[hbm] * 11 + [vm, hbm], out_specs=(hbm, hbm, vm, vm), scratch_shapes=scratch,
        compiler_params=pltpu.CompilerParams(collective_id=cid, has_side_effects=True, vmem_limit_bytes=63 << 20), name="backward")(*args)

def finish_kernel(red, tot, y, dx, y_o, dx_o, gain, bias, qkv, qb, out, ob, up, ub, down, db, wide):
    y_o[...] = y[...]
    dx_o[...] = dx[...]
    wide[...] = tot[...].astype(f32)
    unpack_vectors(wide, gain, bias, qb, ob, ub, db)
    for b in range(8):
        unpack_shard(b, red, qkv, out, up, down)

def outputs(y, dx, red, tot):
    vm = pl.BlockSpec(memory_space=pltpu.VMEM)
    sd = lambda *shape, dt=f32: jax.ShapeDtypeStruct(shape, dt)
    outs = (sd(4, 64, D, dt=bf16), sd(4, 64, D, dt=bf16), sd(2, 3, 24), sd(2, 3, 24), sd(2, 2, 24, 3 * D), sd(2, 2, 2, 24), sd(2, 2, 24, D), sd(2, 2, 24), sd(2, 24, F), sd(2, 96), sd(2, 96, D), sd(2, 24))
    return pl.pallas_call(finish_kernel, out_shape=outs, in_specs=[vm] * 4, out_specs=tuple([vm] * 12), scratch_shapes=[pltpu.VMEM((32, 128), f32)],
        compiler_params=pltpu.CompilerParams(vmem_limit_bytes=40 << 20), name="outputs")(red, tot, y, dx)


def local(clips, *rest):
    y, dx, *grads = outputs(*backward(*forward(clips[0], *rest[:-1], rest[-1][0])))
    return (y[None], dx[None]) + tuple(grads)

def solution(mesh):
    f = P("fsdp", "seq", None, None)
    ins = (f, P(None, None, "fsdp"), P(None, None, "fsdp"), P(None, None, "fsdp", None), P(None, None, None, "fsdp"), P(None, None, "fsdp", None),
        P(None, None, "fsdp"), P(None, "fsdp", None), P(None, "fsdp"), P(None, "fsdp", None), P(None, "fsdp"), f)
    return jax.shard_map(local, mesh=mesh, in_specs=ins, out_specs=(f, f) + ins[1:11], check_vma=False)
```

```python
import functools
import jax
import jax.numpy as jnp
from jax import lax
from jax.experimental import pallas as pl
from jax.experimental.pallas import tpu as pltpu
from jax.sharding import PartitionSpec as P
MESH = pl.DeviceIdType.MESH
bf16, f32 = jnp.bfloat16, jnp.float32
T, D, F = 256, 768, 3072
NN = (((1,), (0,)), ((), ()))
NT = (((1,), (1,)), ((), ()))
ORDERS = (("x", "y", "z"), ("y", "z", "x"), ("z", "x", "y"))
STORED = ("x", "z", "y")

def coords():
    f, s = lax.axis_index("fsdp"), lax.axis_index("seq")
    return {"x": f // 8, "y": f % 4, "z": ((f // 4) % 2) * 2 + s // 2}, s % 2

def dev(at, c):
    return (at["x"] * 8 + (at["z"] // 2) * 4 + at["y"], (at["z"] % 2) * 2 + c)

def moved(at, axis, by):
    return {**at, axis: (at[axis] + by + 4) % 4}

def greet(at, c):
    bar = pltpu.get_barrier_semaphore()
    other = moved(at, "z", 1 - 2 * (at["z"] % 2))
    peers = [dev(moved(at, a, d), c) for a in "xyz" for d in (1, -1)] + [dev(at, 1 - c), dev(other, 1 - c)]
    for p in peers:
        pl.semaphore_signal(bar, inc=1, device_id=p, device_id_type=MESH)
    pl.semaphore_wait(bar, len(peers))

def remote(src, dst, ssem, rsem, to):
    return pltpu.make_async_remote_copy(src, dst, ssem, rsem, device_id=to, device_id_type=MESH)

def index(sel):
    return tuple(pl.ds(0, 4) if v is None else pl.ds(*v) if isinstance(v, tuple) else v for v in sel)

class Gather:
    ROUNDS = 8
    def __init__(self, s, g, b, p, at, c, sems):
        self.s, self.g, self.b, self.p, self.at, self.c = s, g, b, p, at, c
        self.ssem, self.rsem, self.lsem = sems
        self.order, self.pending = ORDERS[p], []
    def ref(self, st, coord, half=None, c=None):
        sel = {}
        for i, a in enumerate(self.order):
            sel[a] = None if i < st else coord if i == st else self.at[a]
        if half is not None and st > 0:
            sel[[a for a in STORED if a in self.order[:st]][0]] = (2 * half, 2)
        ref = self.g.at[(self.b, self.c if c is None else c, self.p) + index(sel[a] for a in STORED)]
        return ref if half is None or st > 0 else ref.at[pl.ds(32 * half, 32 - 16 * half), :]
    def copy(self, src, dst, k, to):
        return remote(src, dst, self.ssem.at[self.b, self.p, k], self.rsem.at[self.b, self.p, k], to)
    def go(self, ref, k, to, src=None):
        cp = self.copy(ref if src is None else src, ref, k, to)
        cp.start()
        self.pending.append(cp)
    def got(self, ref, k):
        self.copy(ref, ref, k, dev(self.at, 1 - self.c)).wait_recv()
    def round(self, r):
        sib = dev(self.at, 1 - self.c)
        last = self.at[self.order[2]]
        if 0 < r < 7:
            st, ph = divmod(r - 1, 2)
            here = self.at[self.order[st]]
            if ph == 0:
                self.got(self.ref(st, (here + 3) % 4), 4 * st)
                self.got(self.ref(st, (here + 1) % 4), 4 * st + 1)
            else:
                for h in (0, 1):
                    self.got(self.ref(st, (here + 2) % 4, h), 4 * st + 2 + h)
        if r < 6:
            st, ph = divmod(r, 2)
            a = self.order[st]
            here = self.at[a]
            up, down = (dev(moved(self.at, a, d), self.c) for d in (1, -1))
            own = self.ref(st, here)
            if ph == 0:
                src = None
                if r == 0:
                    src = self.s.at[self.b, self.c, self.p, self.at["z"] % 2]
                    self.local = pltpu.make_async_copy(src, own, self.lsem.at[self.b, self.p])
                    self.local.start()
                if r == 2:
                    self.local.wait()
                self.go(own, 4 * st, up, src)
                self.go(own, 4 * st + 1, down, src)
                if st == 2:
                    self.go(own, 12, sib)
            else:
                self.go(self.ref(st, (here + 3) % 4, 0), 4 * st + 2, up)
                self.go(self.ref(st, (here + 1) % 4, 1), 4 * st + 3, down)
                if st == 2:
                    self.go(self.ref(2, (here + 3) % 4), 13, sib)
                    self.go(self.ref(2, (here + 1) % 4), 14, sib)
        if r == 6:
            self.go(self.ref(2, (last + 2) % 4), 15, sib)
        if r == 7:
            for k, by in ((12, 0), (13, 3), (14, 1), (15, 2)):
                self.got(self.ref(2, (last + by) % 4, c=1 - self.c), k)
    def end(self):
        for cp in self.pending:
            cp.wait_send()

class Point:
    def __init__(self, at, c, ssem, rsem):
        self.at, self.c, self.ssem, self.rsem, self.sends = at, c, ssem, rsem, []
    def send(self, src, dst, k, to):
        cp = remote(src, dst, self.ssem.at[k], self.rsem.at[k], to)
        cp.start()
        self.sends.append(cp)
    def got(self, ref, k):
        remote(ref, ref, self.ssem.at[k], self.rsem.at[k], dev(self.at, 1 - self.c)).wait_recv()
    def near(self, a, d):
        return dev(moved(self.at, a, d), self.c)
    def end(self):
        for cp in self.sends:
            cp.wait_send()

class SmallGather(Point):
    def __init__(self, s, gs, at, c, ssem, rsem, lsem):
        super().__init__(at, c, ssem, rsem)
        self.s, self.gs, self.lsem = s, gs, lsem
    def round(self, r):
        at, gs = self.at, self.gs
        x, y, zh = at["x"], at["y"], at["z"] // 2
        blk = lambda by: gs.at[(x + by + 4) % 4, zh, y]
        row = lambda by: gs.at[:, zh, (y + by + 4) % 4]
        if r == 0:
            self.local = pltpu.make_async_copy(self.s, blk(0), self.lsem)
            self.local.start()
            self.send(self.s, blk(0), 0, self.near("x", 1))
            self.send(self.s, blk(0), 1, self.near("x", -1))
        if r == 1:
            self.got(blk(-1), 0)
            self.send(blk(-1), blk(-1), 2, self.near("x", 1))
        if r == 2:
            self.got(blk(1), 1)
            self.got(blk(2), 2)
            self.local.wait()
            self.send(row(0), row(0), 3, self.near("y", 1))
            self.send(row(0), row(0), 4, self.near("y", -1))
        if r == 3:
            self.got(row(-1), 3)
            self.send(row(-1), row(-1), 5, self.near("y", 1))
        if r == 4:
            self.got(row(1), 4)
            self.got(row(2), 5)
            self.send(gs.at[:, zh], gs.at[:, zh], 6, dev({**at, "z": 3 - at["z"]}, self.c))
        if r == 5:
            self.got(gs.at[:, 1 - zh], 6)

class Reduce:
    def __init__(self, n, b, at, c, made, red, held, land, sums, sems):
        self.n, self.b, self.at, self.c = n, b, at, c
        self.made, self.red, self.held, self.land = made.at[n % made.shape[0]], red, held.at[n % held.shape[0]], land
        self.sums = [self.made.at[c]] + [q.at[n % q.shape[0]] for q in sums]
        self.ssem, self.rsem, self.lsem = sems
        self.sib = dev(at, 1 - c)
        self.pending = {}
    def block(self, p, st, by, half=None, base=None):
        order = ORDERS[p][::-1]
        sel = {a: None for a in STORED if a not in order[:st]}
        sel[order[st]] = (self.at[order[st]] + by + 4) % 4
        if half is not None and st < 2:
            sel[[a for a in sel if a != order[st]][0]] = (2 * half, 2)
        ref = (self.sums[st] if base is None else base).at[(p,) + index(sel.values())]
        return ref.at[pl.ds(32 * half, 32 - 16 * half), :] if half is not None and st == 2 else ref
    def arrival(self, p, st, k, half=None):
        if half is None:
            ref = self.land[st][0]
            return ref.at[self.n % ref.shape[0], p, k]
        ref = self.land[st][1]
        ref = ref.at[self.n % ref.shape[0], p]
        return ref.at[pl.ds(2 * half, 2)] if st < 2 else ref.at[pl.ds(32 * half, 32 - 16 * half), :]
    def copy(self, src, dst, p, k, to):
        return remote(src, dst, self.ssem.at[self.b, p, k], self.rsem.at[self.b, p, k], to)
    def send(self, group, *a):
        cp = self.copy(*a)
        cp.start()
        self.pending.setdefault(group, []).append(cp)
    def got(self, ref, p, k):
        self.copy(ref, ref, p, k, self.sib).wait_recv()
    def sent(self, group):
        for cp in self.pending.pop(group, []):
            cp.wait_send()
    def near(self, p, st, by):
        return dev(moved(self.at, ORDERS[p][2 - st], by), self.c)
    def halves(self, st, p):
        self.send(st, self.block(p, st, 2, 0), self.arrival(p, st, 2, 0), p, 4 * st + 0, self.near(p, st, 1))
        self.send(st, self.block(p, st, 2, 1), self.arrival(p, st, 2, 1), p, 4 * st + 1, self.near(p, st, -1))
    def give(self):
        for i, by in enumerate((2, 1, -1, 0)):
            for p in range(3):
                src = self.block(p, 0, by, base=self.made.at[1 - self.c])
                self.send(0, src, self.block(p, 0, by, base=self.held), p, 12 + i, self.sib)
    def add_held(self, p, by, i):
        mine, held = self.block(p, 0, by), self.block(p, 0, by, base=self.held)
        self.got(held, p, 12 + i)
        mine[...] = mine[...] + held[...]
    def take(self):
        for p in range(3):
            self.add_held(p, 2, 0)
            self.halves(0, p)
        for i, by in ((1, 1), (2, -1), (3, 0)):
            for p in range(3):
                self.add_held(p, by, i)
    def add_halves(self, st):
        for p in range(3):
            for half, by in ((0, 1), (1, -1)):
                dst, src = self.block(p, st, by, half), self.arrival(p, st, 2, half)
                self.got(src, p, 4 * st + half)
                dst[...] = dst[...] + src[...]
    def wholes(self, st):
        for p in range(3):
            self.send(st, self.block(p, st, 1), self.arrival(p, st, 0), p, 4 * st + 2, self.near(p, st, 1))
            self.send(st, self.block(p, st, -1), self.arrival(p, st, 1), p, 4 * st + 3, self.near(p, st, -1))
    def add_wholes(self, st):
        for p in range(3):
            s0, s1 = self.arrival(p, st, 0), self.arrival(p, st, 1)
            self.got(s0, p, 4 * st + 2)
            self.got(s1, p, 4 * st + 3)
            total = self.block(p, st, 0)[...].astype(f32) + s0[...].astype(f32) + s1[...].astype(f32)
            self.sums[st + 1][p] = total.astype(bf16)
            if st < 2:
                self.halves(st + 1, p)
    def peers(self):
        other = moved(self.at, "z", 1 - 2 * (self.at["z"] % 2))
        zl = self.at["z"] % 2
        return ((dev(other, self.c), self.c, 1 - zl), (dev(other, 1 - self.c), 1 - self.c, 1 - zl), (self.sib, 1 - self.c, zl))
    def share(self):
        own, mine = self.sums[3], self.red.at[self.b, self.c, :, self.at["z"] % 2]
        self.local = pltpu.make_async_copy(own, mine, self.lsem.at[self.b])
        self.local.start()
        for i, (to, _, _) in enumerate(self.peers()):
            self.send(3, own, mine, i, 16, to)
    def collect(self):
        self.local.wait()
        for i, (_, c, zl) in enumerate(self.peers()):
            self.got(self.red.at[self.b, c, :, zl], i, 16)
    def end(self):
        for g in list(self.pending):
            self.sent(g)

class SmallReduce(Point):
    def __init__(self, sg, tot, bx, by, bz, at, c, ssem, rsem):
        super().__init__(at, c, ssem, rsem)
        self.sg, self.tot, self.bx, self.by, self.bz = sg, tot, bx, by, bz
    def round(self, r):
        at, sg, tot, bx, by, bz = self.at, self.sg, self.tot, self.bx, self.by, self.bz
        x, y, z = at["x"], at["y"], at["z"]
        zh, zl = z // 2, z % 2
        blk = lambda d: sg.at[(x + d + 4) % 4]
        row = lambda d: sg.at[x, :, (y + d + 4) % 4]
        def add(dst, *more):
            v = dst[...].astype(f32)
            for q in more:
                v = v + q[...].astype(f32)
            dst[...] = v.astype(bf16)
        if r == 0:
            self.send(blk(2), bx.at[0], 0, self.near("x", 1))
            self.send(blk(-1), bx.at[1], 1, self.near("x", -1))
        if r == 1:
            self.got(bx.at[0], 0)
            add(blk(1), bx.at[0])
            self.send(blk(1), bx.at[2], 2, self.near("x", 1))
        if r == 2:
            self.got(bx.at[1], 1)
            self.got(bx.at[2], 2)
            add(blk(0), bx.at[1], bx.at[2])
            self.send(row(2), by.at[0], 3, self.near("y", 1))
            self.send(row(-1), by.at[1], 4, self.near("y", -1))
        if r == 3:
            self.got(by.at[0], 3)
            add(row(1), by.at[0])
            self.send(row(1), by.at[2], 5, self.near("y", 1))
        if r == 4:
            self.got(by.at[1], 4)
            self.got(by.at[2], 5)
            add(row(0), by.at[1], by.at[2])
            self.send(sg.at[x, 1 - zh, y], bz.at[0], 6, dev({**at, "z": 3 - z}, self.c))
        if r == 5:
            self.got(bz.at[0], 6)
            tot[0] = (sg[x, zh, y].astype(f32) + bz[0].astype(f32)).astype(bf16)
            self.send(tot.at[0], bz.at[1], 7, self.near("z", 1 - 2 * zl))
        if r == 6:
            self.got(bz.at[1], 7)
            tot[1] = (tot[0].astype(f32) + bz[1].astype(f32)).astype(bf16)
            self.send(tot.at[1], bz.at[2], 8, dev(at, 1 - self.c))
        if r == 7:
            self.got(bz.at[2], 8)
            tot[2] = (tot[1].astype(f32) + bz[2].astype(f32)).astype(bf16)

def exchange(n, src, dst, to_places, sems):
    f, s = lax.axis_index("fsdp"), lax.axis_index("seq")
    ssem, rsem, lsem = sems
    cps = []
    for i in (2, 3, 1, 0):
        t = (s + i) % 4
        if to_places:
            a, b = src.at[:, pl.ds(pl.multiple_of(t * 16, 16), 16), :], dst.at[pl.ds(4 * s, 4)]
        else:
            a, b = src.at[pl.ds(4 * t, 4)], dst.at[:, pl.ds(pl.multiple_of(s * 16, 16), 16), :]
        cp = pltpu.make_async_copy(a, b, lsem.at[n]) if i == 0 else remote(a, b, ssem.at[n, i - 1], rsem.at[n, i - 1], (f, t))
        cp.start()
        cps.append(cp)
    return cps

def finish(cps):
    for cp in cps:
        cp.wait()

def dot(a, b, dims=NN):
    return lax.dot_general(a, b, dims, preferred_element_type=f32)

def iota(shape, dim):
    return lax.broadcasted_iota(jnp.int32, shape, dim)

def chunk_at(m):
    return m // 6, (m // 2) % 3, m % 2

def cols(n, w=256):
    return slice(w * n, w * n + w)

def stats(x):
    xc = x - jnp.mean(x, axis=-1, keepdims=True)
    r = lax.rsqrt(jnp.mean(xc * xc, axis=-1, keepdims=True) + 1e-6)
    return xc * r, r

def norm_rows(u, gain, bias, a):
    for i in range(8):
        at = cols(i, 32)
        n, _ = stats(u[at, :].astype(f32))
        a[at, :] = (n * gain + bias).astype(bf16)

def norm_back(u, gain, da, du):
    sg = sb = jnp.zeros((8, D), f32)
    for i in range(8):
        at = cols(i, 32)
        n, r = stats(u[at, :].astype(f32))
        d = da[at, :]
        sg = sg + jnp.sum((d * n).reshape(4, 8, D), axis=0)
        sb = sb + jnp.sum(d.reshape(4, 8, D), axis=0)
        dn = d * gain
        c1 = jnp.mean(dn, axis=-1, keepdims=True)
        c2 = jnp.mean(dn * n, axis=-1, keepdims=True)
        du[at, :] = du[at, :] + r * (dn - c1 - n * c2)
    return jnp.sum(sg, axis=0, keepdims=True), jnp.sum(sb, axis=0, keepdims=True)

def column_sum(x):
    return dot(jnp.ones((8, T), bf16), x)[0:1]

def lanes(h, value):
    return jnp.where(iota((1, 128), 1) // 64 == h, value, 0.0).astype(bf16)

def attend(qkv, mask, o, lse_t, acc):
    lane = iota((1, 128), 1)
    for hp in range(6):
        q, k, v = (qkv[:, cols(6 * i + hp, 128)] for i in range(3))
        mixed = None
        for h in range(2):
            s = dot(q, k * lanes(h, 0.125), NT) + mask[...].astype(f32)
            top = jnp.max(s, axis=-1, keepdims=True)
            e = jnp.exp(s - top)
            tot = jnp.sum(e, axis=-1, keepdims=True)
            part = dot((e * (1.0 / tot)).astype(bf16), v * lanes(h, 1.0))
            mixed = part if mixed is None else mixed + part
            lse = top + jnp.log(tot)
            acc[...] = jnp.where(lane == 2 * hp + h, lse, 0.0 if hp + h == 0 else acc[...])
        o[:, cols(hp, 128)] = mixed.astype(bf16)
    lse_t[...] = acc[...].T[0:16, :]

def attend_back(qkv, mask, lse_t, do, delta_t, g, kt, dqt):
    kt[...] = (qkv[:, D:2 * D].astype(f32) * 0.125).T.astype(bf16)
    for hp in range(6):
        q, k, v = (qkv[:, cols(6 * i + hp, 128)] for i in range(3))
        d = do[:, cols(hp, 128)]
        dk = dv = None
        for h in range(2):
            row = slice(2 * hp + h, 2 * hp + h + 1)
            pt = jnp.exp(dot(k * lanes(h, 0.125), q, NT) + mask[...].astype(f32) - lse_t[row, :])
            dpt = dot(v * lanes(h, 1.0), d, NT)
            dst = (pt * (dpt - delta_t[row, :])).astype(bf16)
            a = dot(pt.astype(bf16), d * lanes(h, 1.0))
            b = dot(dst, q * lanes(h, 0.125))
            dv = a if dv is None else dv + a
            dk = b if dk is None else dk + b
            rows = cols(2 * hp + h, 64)
            dqt[rows, :] = dot(kt[rows, :], dst).astype(bf16)
        g[:, cols(6 + hp, 128)] = dk.astype(bf16)
        g[:, cols(12 + hp, 128)] = dv.astype(bf16)
    g[:, 0:D] = dqt[...].T

def head_sums(do, o, out):
    one = jnp.where(iota((16, D), 1) // 64 == iota((16, D), 0), 1.0, 0.0).astype(bf16)
    x = do[...].astype(f32) * o[...].astype(f32)
    hi = x.astype(bf16)
    lo = (x - hi.astype(f32)).astype(bf16)
    out[...] = dot(one, hi, NT) + dot(one, lo, NT)

def set_masks(masks):
    r0, r1 = iota((T, T), 0), iota((T, T), 1)
    masks[0] = jnp.where(r0 // 64 == r1 // 64, 0.0, -1e30).astype(bf16)
    masks[1] = jnp.where(r0 % 16 == r1 % 16, 0.0, -1e30).astype(bf16)

def spread(gs, vec, upb):
    place = jnp.where((iota((128, D), 1) % 24 == iota((128, D), 0)), 1.0, 0.0).astype(bf16)
    own = iota((32, 1, D), 2) // 24 == iota((32, 1, D), 0)
    place4 = jnp.where((iota((128, F), 1) % 96 == iota((128, F), 0)), 1.0, 0.0).astype(bf16)
    own4 = iota((32, F), 1) // 96 == iota((32, F), 0)
    for l in range(2):
        x = gs[:, :, :, pl.ds(16 * l, 16), :].reshape(32, 16, 128)
        y = dot(x.reshape(512, 128), place).reshape(32, 16, D)
        vec[l] = jnp.sum(jnp.where(own, y, 0.0), axis=0)
        z = dot(x.astype(f32)[:, 13, :].astype(bf16), place4)
        upb[l] = jnp.sum(jnp.where(own4, z, 0.0), axis=0, keepdims=True)

def collect(l, vecg, upg, sg):
    place = jnp.where((iota((D, 128), 0) % 24 == iota((D, 128), 1)), 1.0, 0.0).astype(bf16)
    own = iota((32, 1, D), 2) // 24 == iota((32, 1, D), 0)
    x = jnp.where(own, vecg[l][None], 0.0).astype(bf16).reshape(512, D)
    y = dot(x, place).reshape(32, 16, 128)
    place4 = jnp.where((iota((F, 128), 0) % 96 == iota((F, 128), 1)), 1.0, 0.0).astype(bf16)
    own4 = iota((32, F), 1) // 96 == iota((32, F), 0)
    z = dot(jnp.where(own4, upg[l], 0.0).astype(bf16), place4)
    y = jnp.where(iota((32, 16, 128), 1) == 13, z[:, None, :], y)
    sg[:, :, :, pl.ds(16 * l, 16), :] = y.astype(bf16).reshape(4, 2, 4, 16, 128)

def unpack_chunk(st, w, lo, hi):
    for i in range(16):
        x = st[pl.ds(2 * i, 2)].astype(f32).reshape(2, 2, 24, 128)
        at = cols(i, 48)
        w[at, pl.ds(lo, 128)] = x[:, 0].reshape(48, 128).astype(bf16)
        w[at, pl.ds(hi, 128)] = x[:, 1].reshape(48, 128).astype(bf16)

def pack_pair(r):
    a, b = r[:, :128].reshape(32, 24, 128), r[:, 128:].reshape(32, 24, 128)
    return jnp.concatenate([a, b], axis=1).astype(bf16).reshape(4, 2, 4, 48, 128)

def pair(x, lo, hi):
    return jnp.concatenate([x[:, lo:lo + 128], x[:, hi:hi + 128]], axis=1)

def pack_shard(b, qkv, out, up, down, s):
    l, j = divmod(b, 4)
    for m in range(12):
        if j == 3:
            x = down[l, cols(m % 2, 48), cols(m // 2, 128)]
        else:
            w, n, half = (up.at[l], m, 1536) if j == 2 else (qkv.at[l, j], m, 1152) if m < 9 else (out.at[l, j], m - 9, 384)
            lo, hi = w[:, cols(n, 128)], w[:, half + 128 * n:half + 128 * n + 128]
            x = jnp.concatenate([lo.astype(f32), hi.astype(f32)], axis=0).astype(bf16)
        s[(b,) + chunk_at(m)] = x

def unpack_shard(b, s, qkv, out, up, down):
    l, j = divmod(b, 4)
    for m in range(12):
        y = s[(b,) + chunk_at(m)].astype(f32)
        if j == 3:
            down[l, cols(m % 2, 48), cols(m // 2, 128)] = y
        else:
            w, n, half = (up.at[l], m, 1536) if j == 2 else (qkv.at[l, j], m, 1152) if m < 9 else (out.at[l, j], m - 9, 384)
            w[:, cols(n, 128)] = y[:24]
            w[:, half + 128 * n:half + 128 * n + 128] = y[24:]

def pack_vectors(gain, bias, qb, ob, ub, db, wide, s):
    wide[...] = jnp.zeros_like(wide)
    for l in range(2):
        r = 16 * l
        for i in range(3):
            wide[r + i:r + i + 1, 0:24] = gain[i, l:l + 1].astype(f32)
            wide[r + 3 + i:r + 4 + i, 0:24] = bias[i, l:l + 1].astype(f32)
        for i in range(4):
            wide[r + 6 + i:r + 7 + i, 0:24] = qb[l, i // 2, i % 2:i % 2 + 1].astype(f32)
        wide[r + 10:r + 12, 0:24] = ob[l].astype(f32)
        wide[r + 12:r + 13, 0:24] = db[l:l + 1].astype(f32)
        wide[r + 13:r + 14, 0:96] = ub[l:l + 1].astype(f32)
    s[...] = wide[...].astype(bf16)

def unpack_vectors(wide, gain, bias, qb, ob, ub, db):
    for l in range(2):
        r = 16 * l
        for i in range(3):
            gain[i, l:l + 1] = wide[r + i:r + i + 1, 0:24]
            bias[i, l:l + 1] = wide[r + 3 + i:r + 4 + i, 0:24]
        for i in range(4):
            qb[l, i // 2, i % 2:i % 2 + 1] = wide[r + 6 + i:r + 7 + i, 0:24]
        ob[l] = wide[r + 10:r + 12, 0:24]
        db[l:l + 1] = wide[r + 12:r + 13, 0:24]
        ub[l:l + 1] = wide[r + 13:r + 14, 0:96]


def slot_of(b, r):
    return r + (0, 2, 3, 4, 5, 6, 7, 8)[b]

LAST = slot_of(7, 7)

def forward_kernel(clips, gain_i, bias_i, qkv_i, qb_i, out_i, ob_i, up_i, ub_i, down_i, db_i, cot, gw, wqkv_o, wo_o, wup_o, qkv_o, o_o, lse_o, u_o, u2_o, h_o, gp_o, vec_o, cot_o,
                   s, ss, wide, gs, wqkv, wo, wup, wdn, stage, su, sqkv, so, slse, su2, sh, sgp, vec, upb, masks, a_buf, acc, x3f, x3p, rp, rf,
                   gss, grs, gls, sss, srs, sls, ess, ers, els, wsem, osem):
    at, c = coords()
    greet(at, c)
    small = SmallGather(ss, gs, at, c, sss, srs, sls.at[0])
    parts = [[Gather(s, gw, b, p, at, c, (gss, grs, gls)) for p in range(3)] for b in range(8)]
    state = {"t": 0, "out": 0}
    halfway, ready, fetched, unpacked, done = set(), set(), set(), set(), set()
    esems = (ess, ers, els)
    saves = {}

    def save(key, src, dst):
        cp = pltpu.make_async_copy(src, dst, osem.at[state["out"]])
        state["out"] += 1
        cp.start()
        saves[key] = cp

    def chunk_copy(b, m, ci, p, zl):
        gz = gw.reshape(8, 2, 3, 4, 2, 2, 4, 48, 128)
        dst = stage.at[b % 2, m] if b % 4 < 3 else wdn.at[:, :, :, m % 2, :, pl.ds(128 * (m // 2), 128)]
        return pltpu.make_async_copy(gz.at[b, ci, p, :, :, zl], dst, wsem.at[b % 2, m])

    def fetch(b, part):
        if b % 4 == 3:
            for m in range(12) if part == 1 else ():
                chunk_copy(b, m, *chunk_at(m)).start()
            return
        ci = c if part == 0 else 1 - c
        for i in range(6):
            chunk_copy(b, 6 * ci + i, ci, i // 2, i % 2).start()

    def try_fetch():
        for b in range(7):
            if (b < 2 or b - 2 in unpacked) and (b % 4 < 3 or b < 4 or b - 4 in done):
                for part, there in ((0, halfway), (1, ready)):
                    if b in there and (b, part) not in fetched:
                        fetched.add((b, part))
                        fetch(b, part)

    def slot():
        t = state["t"]
        if t > LAST:
            return
        if t == 0:
            pack_vectors(gain_i, bias_i, qb_i, ob_i, ub_i, db_i, wide, ss)
        if t < 6:
            small.round(t)
        for b in range(8) if t == 0 else reversed(range(8)):
            for r in range(8):
                if slot_of(b, r) == t:
                    if r == 0:
                        pack_shard(b, qkv_i, out_i, up_i, down_i, s)
                    for p in range(3):
                        parts[b][p].round(r)
                    if r == 6:
                        halfway.add(b)
                        try_fetch()
                    if r == 7:
                        ready.add(b)
                        try_fetch()
        state["t"] += 1

    def poll(b):
        if b < 7 and state["t"] <= slot_of(b + 1, 7):
            slot()

    def weights(b):
        if b in unpacked:
            return
        l, j = divmod(b, 4)
        while b not in ready:
            slot()
        try_fetch()
        if j < 3 and l:
            saves.pop((0, j)).wait()
            if j < 2:
                saves.pop((0, j, 0)).wait()
        for m in range(12):
            chunk_copy(b, m, *chunk_at(m)).wait()
            if j == 3:
                continue
            st = stage.at[b % 2, m].reshape(32, 48, 128)
            if j == 2:
                unpack_chunk(st, wup, 128 * m, 1536 + 128 * m)
            elif m < 9:
                unpack_chunk(st, wqkv.at[j], 128 * m, 1152 + 128 * m)
            else:
                unpack_chunk(st, wo.at[j], 128 * (m - 9), 384 + 128 * (m - 9))
        unpacked.add(b)
        try_fetch()
        if j < 2:
            save((l, j), wqkv.at[j], wqkv_o.at[l, j])
            save((l, j, 0), wo.at[j], wo_o.at[l, j])
        elif j == 2:
            save((l, j), wup, wup_o.at[l])

    def branch(l, k, put):
        b = 4 * l + k
        weights(b)
        u, v = su.at[l, k], vec.at[l]
        norm_rows(u, v[k:k + 1], v[3 + k:4 + k], a_buf)
        save(("u", l, k), u, u_o.at[l, k])
        for n in range(9):
            y = dot(a_buf[...], wqkv[k, :, cols(n)])
            if n // 3 != 1:
                y = y + v[6 + 2 * k + n // 6:7 + 2 * k + n // 6, cols(n % 3)]
            sqkv[l, k, :, cols(n)] = y.astype(bf16)
        save(("q", l, k), sqkv.at[l, k], qkv_o.at[l, k])
        poll(b)
        attend(sqkv.at[l, k], masks.at[k], so.at[l, k], slse.at[l, k], acc)
        save(("o", l, k), so.at[l, k], o_o.at[l, k])
        for n in range(3):
            put(n, u[:, cols(n)].astype(f32) + dot(so[l, k], wo[k, :, cols(n)]) + v[10 + k:11 + k, cols(n)])
        done.add(b)

    def layer(l):
        def put1(n, y):
            x3f[l, :, :, cols(n)] = y.astype(bf16).reshape(4, 64, 256)
        branch(l, 0, put1)
        cps = exchange(1 + 2 * l, x3f.at[l], rp.at[1 + l], True, esems)
        weights(4 * l + 1)
        finish(cps)
        su[l, 1] = rp[1 + l].reshape(T, D)
        def put2(n, y):
            su2[l, :, cols(n)] = y
        branch(l, 1, put2)
        save(("u2", l), su2.at[l], u2_o.at[l])
        poll(4 * l + 1)
        weights(4 * l + 2)
        v = vec.at[l]
        norm_rows(su2.at[l], v[2:3], v[5:6], a_buf)
        for n in range(12):
            z = dot(a_buf[...], wup[:, cols(n)]) + upb[l, :, cols(n)]
            cdf = 0.5 * (1.0 + lax.erf(z * 0.7071067811865476))
            sh[l, :, cols(n)] = (z * cdf).astype(bf16)
            sgp[l, :, cols(n)] = (cdf + z * (0.3989422804014327 * jnp.exp(-0.5 * z * z))).astype(bf16)
            if n == 5:
                poll(4 * l + 2)
        save(("h", l), sh.at[l], h_o.at[l])
        save(("gp", l), sgp.at[l], gp_o.at[l])
        done.add(4 * l + 2)
        if l == 1:
            return
        poll(2)
        weights(3)
        for n in range(3):
            y = su2[l, :, cols(n)] + dot(sh[l], wdn[:, :, :, :, :, cols(n)].reshape(F, 256)) + v[12:13, cols(n)]
            x3p[:, :, cols(n)] = y.astype(bf16).reshape(16, 16, 256)
        done.add(3)
        cps = exchange(2, x3p, rf, False, esems)
        weights(4)
        finish(cps)
        su[1, 0] = rf[...].reshape(T, D)

    slot()
    first = exchange(0, cot, rp.at[0], True, esems)
    set_masks(masks)
    su[0, 0] = clips[...].reshape(T, D)
    for _ in range(5):
        slot()
    spread(gs, vec, upb)
    save("vec", vec, vec_o)
    layer(0)
    finish(first)
    save("cot", rp.at[0], cot_o)
    layer(1)
    save("lse", slse, lse_o)
    while 7 not in ready:
        slot()
    for ps in parts:
        for g in ps:
            g.end()
    small.end()
    for cp in saves.values():
        cp.wait()

def forward(*args, cid=0):
    V = pltpu.VMEM
    S = lambda *shape: pltpu.SemaphoreType.DMA(shape)
    vm, hbm = pl.BlockSpec(memory_space=pltpu.VMEM), pl.BlockSpec(memory_space=pl.ANY)
    o = lambda *shape, dt=bf16: jax.ShapeDtypeStruct(shape, dt)
    outs = (o(8, 2, 3, 4, 4, 4, 48, 128), o(2, 2, D, 3 * D), o(2, 2, D, D), o(2, D, F),
            o(2, 2, T, 3 * D), o(2, 2, T, D), o(2, 2, 16, T, dt=f32), o(2, 2, T, D), o(2, T, D, dt=f32), o(2, T, F), o(2, T, F),
            o(2, 16, D, dt=f32), o(16, 16, D))
    scratch = [
        V((8, 2, 3, 2, 48, 128), bf16), V((32, 128), bf16), V((32, 128), f32), V((4, 2, 4, 32, 128), bf16), V((2, D, 3 * D), bf16), V((2, D, D), bf16), V((D, F), bf16), V((4, 2, 4, 2, 48, D), bf16),
        V((2, 12, 4, 2, 4, 48, 128), bf16), V((2, 2, T, D), bf16), V((2, 2, T, 3 * D), bf16), V((2, 2, T, D), bf16), V((2, 2, 16, T), f32),
        V((2, T, D), f32), V((2, T, F), bf16), V((2, T, F), bf16), V((2, 16, D), f32), V((2, 1, F), f32), V((2, T, T), bf16),
        V((T, D), bf16), V((T, 128), f32), V((2, 4, 64, D), bf16), V((16, 16, D), bf16), V((3, 16, 16, D), bf16), V((4, 64, D), bf16),
        S(8, 3, 16), S(8, 3, 16), S(8, 3), S(7), S(7), S(1), S(4, 3), S(4, 3), S(4), S(2, 12), S(40)]
    return pl.pallas_call(forward_kernel, out_shape=outs, in_specs=[vm] * 12, out_specs=tuple([hbm] * 13), scratch_shapes=scratch,
        compiler_params=pltpu.CompilerParams(collective_id=cid, has_side_effects=True, vmem_limit_bytes=63 << 20), name="forward")(*args)


def backward_kernel(gw, wqkv_i, wo_i, wup_i, qkv_i, o_i, lse_i, u_i, u2_i, h_i, gp_i, vec, cot_i, out, dclips, red, total,
                    wqkv, wo, wup, wdn, sqkv, so, slse, su, su2, sh, sgp, masks, a_buf, t_buf, e_buf, g_buf, da, du, dqt, delta,
                    vecg, upg, made_g, tot, x3p, x3f, rf, rp, held, f0, h0, f1, h1, f2, h2, s1, s2, s3, sg, bx, by, bz,
                    rss, rrs, rls, sss, srs, ess, ers, els, isem, osem):
    at, c = coords()
    greet(at, c)
    esems = (ess, ers, els)
    slots = made_g.shape[0]
    grads = made_g.reshape(slots, 2, 3, 4, 2, 2, 4, 48, 128)
    subs = [Reduce(n, 7 - n, at, c, made_g, red, held, ((f0, h0), (f1, h1), (f2, h2)), (s1, s2, s3), (rss, rrs, rls)) for n in range(8)]
    small = SmallReduce(sg, tot, bx, by, bz, at, c, sss, srs)
    state = {"t": 0, "in": 0}
    loads = {}

    def slot():
        t = state["t"]
        state["t"] += 1
        step = {t - n: subs[n] for n in range(8) if 1 <= t - n <= 8}
        if 2 in step:
            step[2].add_halves(0)
        if 1 in step:
            step[1].take()
        if 2 in step:
            step[2].wholes(0)
        if 8 in step:
            step[8].collect()
        for st in (2, 1, 0):
            if 2 * st + 4 in step and st < 2:
                step[2 * st + 4].add_halves(st + 1)
                step[2 * st + 4].wholes(st + 1)
            if 2 * st + 3 in step:
                q = step[2 * st + 3]
                if q.n >= 2:
                    subs[q.n - 2].sent(st + 1)
                q.add_wholes(st)
                if st == 2:
                    q.share()

    def load(key, src, dst):
        cp = pltpu.make_async_copy(src, dst, isem.at[state["in"]])
        state["in"] += 1
        cp.start()
        loads.setdefault(key, []).append(cp)

    def have(key):
        for cp in loads.pop(key, []):
            cp.wait()

    def load_mlp(l):
        load((l, "h"), h_i.at[l], sh)
        gz = gw.reshape(8, 2, 3, 4, 2, 2, 4, 48, 128)
        for m in range(12):
            ci, p, zl = chunk_at(m)
            load((l, "dn"), gz.at[4 * l + 3, ci, p, :, :, zl], wdn.at[:, :, :, m % 2, :, pl.ds(128 * (m // 2), 128)])
        if l == 1:
            load((l, "gp"), gp_i.at[l], sgp)
            load((l, "up"), wup_i.at[l], wup)
        load((l, "u2"), u2_i.at[l], su2)

    def load_branch(l, k):
        load((l, k, "w"), wo_i.at[l, k], wo.at[k])
        load((l, k, "q"), qkv_i.at[l, k], sqkv.at[k])
        load((l, k, "q"), o_i.at[l, k], so.at[k])
        load((l, k, "w"), wqkv_i.at[l, k], wqkv.at[k])
        load((l, k, "q"), u_i.at[l, k], su.at[k])

    def claim(b):
        n = 7 - b
        while state["t"] <= n:
            slot()
        if n >= slots:
            subs[n - slots].sent(0)

    def put(b, m, value, x=None):
        ci, p, zl = chunk_at(m)
        if x is None:
            grads[(7 - b) % slots, ci, p, :, :, zl] = value
        else:
            grads[(7 - b) % slots, ci, p, x, :, zl] = value

    def made(b):
        subs[7 - b].give()

    def mlp(l):
        v = vec.at[l]
        e = e_buf.at[0]
        e[...] = du[...].astype(bf16)
        if l == 1:
            mlp_down_grads(l)
        have((l, "dn"))
        have((l, "gp"))
        for i in range(8):
            w = wdn[i // 2, i % 2].reshape(384, D)
            sgp[:, cols(i, 384)] = (dot(e[...], w, NT) * sgp[:, cols(i, 384)].astype(f32)).astype(bf16)
        have((l, "up"))
        for n in range(3):
            da[:, cols(n)] = dot(sgp[...], wup[cols(n), :], NT)
        have((l, "u2"))
        dg, db = norm_back(su2, v[2:3], da, du)
        vecg[l, 2:3, :] = dg
        vecg[l, 5:6, :] = db
        if l == 0:
            mlp_down_grads(l)

    def mlp_down_grads(l):
        e = e_buf.at[0]
        have((l, "h"))
        claim(4 * l + 3)
        for i in range(4):
            t_buf[...] = sh[:, cols(i, 768)].T
            for n in range(3):
                r = dot(t_buf[...], e[:, cols(n)]).astype(bf16).reshape(2, 4, 2, 48, 256)
                for q in range(4):
                    put(4 * l + 3, 4 * n + q, r[:, :, q % 2, :, cols(q // 2, 128)], i)
        vecg[l, 12:13, :] = column_sum(e[...])
        made(4 * l + 3)

    def mlp_up_grads(l):
        v = vec.at[l]
        norm_rows(su2, v[2:3], v[5:6], a_buf)
        t_buf[...] = a_buf[...].T
        claim(4 * l + 2)
        for m in range(12):
            put(4 * l + 2, m, pack_pair(dot(t_buf[...], pair(sgp, 128 * m, 1536 + 128 * m))))
        made(4 * l + 2)
        upg[l] = column_sum(sgp[...])

    def branch(l, k):
        v = vec.at[l]
        e = e_buf.at[k]
        e[...] = du[...].astype(bf16)
        have((l, k, "w"))
        have((l, k, "q"))
        for n in range(3):
            a_buf[:, cols(n)] = dot(e[...], wo[k, cols(n), :], NT).astype(bf16)
        head_sums(a_buf, so.at[k], delta)
        attend_back(sqkv.at[k], masks.at[k], slse.at[l, k], a_buf, delta, g_buf, t_buf, dqt)
        if l + k == 0:
            branch_grads(0, 0)
        if (l, k) == (0, 1):
            mlp_up_grads(0)
        for n in range(3):
            da[:, cols(n)] = dot(g_buf[...], wqkv[k, cols(n), :], NT)
        dg, db = norm_back(su.at[k], v[k:k + 1], da, du)
        vecg[l, k:k + 1, :] = dg
        vecg[l, 3 + k:4 + k, :] = db

    def branch_grads(l, k):
        v = vec.at[l]
        e = e_buf.at[k]
        claim(4 * l + k)
        t_buf[...] = so[k].T
        for i in range(3):
            put(4 * l + k, 9 + i, pack_pair(dot(t_buf[...], pair(e, 128 * i, 384 + 128 * i))))
        norm_rows(su.at[k], v[k:k + 1], v[3 + k:4 + k], a_buf)
        t_buf[...] = a_buf[...].T
        for m in range(9):
            put(4 * l + k, m, pack_pair(dot(t_buf[...], pair(g_buf, 128 * m, 1152 + 128 * m))))
        made(4 * l + k)
        vecg[l, 10 + k:11 + k, :] = column_sum(e[...])
        vecg[l, 6 + 2 * k:7 + 2 * k, :] = column_sum(g_buf[:, 0:D])
        vecg[l, 7 + 2 * k:8 + 2 * k, :] = column_sum(g_buf[:, 2 * D:3 * D])

    load(("du",), cot_i, rp)
    load_mlp(1)
    load(("lse",), lse_i, slse)
    load_branch(1, 1)
    load_branch(1, 0)
    set_masks(masks)
    vecg[...] = jnp.zeros_like(vecg)
    have(("du",))
    du[...] = rp[...].reshape(T, D).astype(f32)
    have(("lse",))
    for l in (1, 0):
        mlp(l)
        if l == 1:
            mlp_up_grads(1)
            load((0, "gp"), gp_i.at[0], sgp)
            load((0, "up"), wup_i.at[0], wup)
        branch(l, 1)
        x3p[...] = du[...].astype(bf16).reshape(16, 16, D)
        cps = exchange(1 + l, x3p, rf, False, esems)
        branch_grads(l, 1)
        if l == 1:
            load_branch(0, 1)
        finish(cps)
        du[...] = rf[...].reshape(T, D).astype(f32)
        branch(l, 0)
        if l == 1:
            x3f[...] = du[...].astype(bf16).reshape(4, 64, D)
            cps = exchange(3, x3f, rp, True, esems)
            for n in range(3):
                y = su2[:, cols(n)] + dot(sh[...], wdn[:, :, :, :, :, cols(n)].reshape(F, 256)) + vec[1, 12:13, cols(n)]
                x3p[:, :, cols(n)] = y.astype(bf16).reshape(16, 16, 256)
            last = exchange(0, x3p, out, False, esems)
            load_mlp(0)
            branch_grads(l, 0)
            load_branch(0, 0)
            collect(1, vecg, upg, sg)
            finish(cps)
            finish(last)
            du[...] = rp[...].reshape(T, D).astype(f32)
    collect(0, vecg, upg, sg)
    x3f[...] = du[...].astype(bf16).reshape(4, 64, D)
    last = [pltpu.make_async_copy(x3f, dclips, osem.at[0])]
    last[0].start()
    for r in range(8):
        small.round(r)
        slot()
    total[...] = tot[2]
    finish(last)
    for s in subs:
        s.end()
    small.end()

def backward(*args, cid=1):
    V = pltpu.VMEM
    S = lambda *shape: pltpu.SemaphoreType.DMA(shape)
    vm, hbm = pl.BlockSpec(memory_space=pltpu.VMEM), pl.BlockSpec(memory_space=pl.ANY)
    sd = lambda *shape, dt=bf16: jax.ShapeDtypeStruct(shape, dt)
    outs = (sd(4, 64, D), sd(4, 64, D), sd(8, 2, 3, 2, 48, 128), sd(32, 128))
    scratch = [
        V((2, D, 3 * D), bf16), V((2, D, D), bf16), V((D, F), bf16), V((4, 2, 4, 2, 48, D), bf16),
        V((2, T, 3 * D), bf16), V((2, T, D), bf16), V((2, 2, 16, T), f32), V((2, T, D), bf16), V((T, D), f32), V((T, F), bf16), V((T, F), bf16),
        V((2, T, T), bf16), V((T, D), bf16), V((D, T), bf16), V((2, T, D), bf16), V((T, 3 * D), bf16), V((T, D), f32), V((T, D), f32), V((D, T), bf16), V((16, T), f32),
        V((2, 16, D), f32), V((2, 1, F), f32), V((3, 2, 3, 4, 4, 4, 48, 128), bf16), V((3, 32, 128), bf16),
        V((16, 16, D), bf16), V((4, 64, D), bf16), V((4, 64, D), bf16), V((16, 16, D), bf16),
        V((2, 3, 4, 4, 4, 48, 128), bf16), V((3, 3, 2, 4, 4, 48, 128), bf16), V((2, 3, 4, 4, 48, 128), bf16), V((2, 3, 2, 4, 48, 128), bf16), V((2, 3, 4, 48, 128), bf16), V((2, 3, 2, 48, 128), bf16), V((2, 3, 48, 128), bf16),
        V((2, 3, 4, 4, 48, 128), bf16), V((2, 3, 4, 48, 128), bf16), V((2, 3, 48, 128), bf16),
        V((4, 2, 4, 32, 128), bf16), V((3, 2, 4, 32, 128), bf16), V((3, 2, 32, 128), bf16), V((3, 32, 128), bf16),
        S(8, 3, 17), S(8, 3, 17), S(8), S(9), S(9), S(4, 3), S(4, 3), S(4), S(64), S(1)]
    return pl.pallas_call(backward_kernel, out_shape=outs, in_specs=[hbm] * 11 + [vm, hbm], out_specs=(hbm, hbm, vm, vm), scratch_shapes=scratch,
        compiler_params=pltpu.CompilerParams(collective_id=cid, has_side_effects=True, vmem_limit_bytes=63 << 20), name="backward")(*args)

def finish_kernel(red, tot, y, dx, y_o, dx_o, gain, bias, qkv, qb, out, ob, up, ub, down, db, wide):
    y_o[...] = y[...]
    dx_o[...] = dx[...]
    wide[...] = tot[...].astype(f32)
    unpack_vectors(wide, gain, bias, qb, ob, ub, db)
    for b in range(8):
        unpack_shard(b, red, qkv, out, up, down)

def outputs(y, dx, red, tot):
    vm = pl.BlockSpec(memory_space=pltpu.VMEM)
    sd = lambda *shape, dt=f32: jax.ShapeDtypeStruct(shape, dt)
    outs = (sd(4, 64, D, dt=bf16), sd(4, 64, D, dt=bf16), sd(3, 2, 24), sd(3, 2, 24), sd(2, 2, 24, 3 * D), sd(2, 2, 2, 24), sd(2, 2, 24, D), sd(2, 2, 24), sd(2, 24, F), sd(2, 96), sd(2, 96, D), sd(2, 24))
    return pl.pallas_call(finish_kernel, out_shape=outs, in_specs=[vm] * 4, out_specs=tuple([vm] * 12), scratch_shapes=[pltpu.VMEM((32, 128), f32)],
        compiler_params=pltpu.CompilerParams(vmem_limit_bytes=63 << 20), name="outputs")(red, tot, y, dx)


def local(clips, gain, bias, *rest):
    turn = lambda q: jnp.transpose(q, (1, 0, 2))
    y, dx, dgain, dbias, *grads = outputs(*backward(*forward(clips[0], turn(gain), turn(bias), *rest[:-1], rest[-1][0])))
    return (y[None], dx[None], turn(dgain), turn(dbias)) + tuple(grads)

def solution(mesh):
    f = P("fsdp", "seq", None, None)
    ins = (f, P(None, None, "fsdp"), P(None, None, "fsdp"), P(None, None, "fsdp", None), P(None, None, None, "fsdp"), P(None, None, "fsdp", None),
        P(None, None, "fsdp"), P(None, "fsdp", None), P(None, "fsdp"), P(None, "fsdp", None), P(None, "fsdp"), f)
    return jax.shard_map(local, mesh=mesh, in_specs=ins, out_specs=(f, f) + ins[1:11], check_vma=False)
```
